256 devices in a mesh: seq: 32 (over z, x), head: 8 (over y, core).
Axes of the slice: x: 4, y: 4, z: 8, core: 2. Of those that a mesh axis runs over, the one named last changes fastest.
Arguments:
- mixer_input: bfloat16 [65536, 5120], P('seq', 'head'), may hold values from -6 to 6
- write_rows: bfloat16 [65536, 128], P(('seq', 'head')), may hold values from -1.796875 to 1.796875
- read_rows: bfloat16 [65536, 128], P(('seq', 'head')), may hold values from -1.796875 to 1.796875
- log_decay: float32 [80, 65536], P('head', 'seq'), may hold values from -2 to 0, as said below
- skip_gain: float32 [80], P('head'), may hold values from 0.25 to 1.75
- reset_offsets: int32 [32, 4], P('seq'), may hold values from 0 to 2048, as said below
- grad_out: bfloat16 [65536, 5120], P('seq', 'head'), may hold values from -6 to 6
Outputs:
- grad_input: bfloat16 [65536, 5120], P('seq', 'head')
- grad_write: float32 [65536, 128], P(('seq', 'head'))
- grad_read: float32 [65536, 128], P(('seq', 'head'))
The draws below stay inside these ranges and needn't reach their ends.
Inputs may be any that keep to these rules, and one draw needn't show every extreme that they name: `log_decay`: every entry is negative. `reset_offsets`: row d lists, in increasing order, the offsets within block d of 2048 tokens at which an episode begins; unused slots hold 2048 and stand after the used ones; some row uses all 4 slots.
All inputs are finite; a program needn't handle non-finite values.
Results may differ from the reference program's by a relative error of at most 0.0055.
Values may be sent and summed in bfloat16 or wider, within the bound.
No kernel may reach another device: no remote copies, remote signals or barrier semaphores. Data moves between devices by JAX's collectives and lax.ppermute only.
A program may use at most 192 MiB of HBM per device.

```python
import jax
import jax.numpy as jnp
from jax import lax

HEADS = 80
HEAD_DIM = 64
STATE = 128
SPAN = 256
TOK_DEV = 2048
RESETS_DEV = 4
SEQ_BLOCKS = 32
JOINED_POSITIONS = 65536


def draw_log_decay(key, part):
    key = jax.random.fold_in(key, 11)
    prng_seed_handles = jax.random.split(key, 7)
    fast_share = 0.5
    fast_heads = jax.random.uniform(prng_seed_handles[0], (HEADS,), jnp.float32) < fast_share
    slow_rate = jnp.exp(jax.random.uniform(prng_seed_handles[1], (HEADS,), jnp.float32, jnp.log(0.1), jnp.log(0.5))) / JOINED_POSITIONS
    fast_rate = jnp.exp(jax.random.uniform(prng_seed_handles[2], (HEADS,), jnp.float32, jnp.log(1.0 / 50.0), jnp.log(1.0 / 30.0)))
    nominal_frequency = jnp.where(fast_heads, fast_rate, slow_rate)
    speedup_multiplier = jnp.exp(jax.random.uniform(prng_seed_handles[3], (HEADS, SEQ_BLOCKS), jnp.float32, jnp.log(0.5), jnp.log(2.0)))
    speedup_multiplier = jnp.repeat(speedup_multiplier, TOK_DEV, axis=1)
    irregularity_level = jax.random.uniform(prng_seed_handles[4], (HEADS, JOINED_POSITIONS), jnp.float32, 0.5, 1.5)
    cluster_offsets = jax.random.randint(prng_seed_handles[5], (3,), 0, JOINED_POSITIONS)
    cluster_keep_share = jax.random.uniform(prng_seed_handles[6], (3,), jnp.float32, 0.6, 0.8)
    cluster_occurrences = jnp.zeros((JOINED_POSITIONS,), jnp.float32).at[cluster_offsets].add(jnp.log(cluster_keep_share))
    return (-nominal_frequency[:, None] * speedup_multiplier * irregularity_level + cluster_occurrences[None, :]).astype(jnp.float32)


def draw_reset_offsets(key, part):
    key = jax.random.fold_in(key, 7)
    prng_seed_handles = jax.random.split(key, 4)
    listed = jax.random.randint(prng_seed_handles[0], (SEQ_BLOCKS,), 1, RESETS_DEV + 1)
    active = jax.random.randint(prng_seed_handles[1], (SEQ_BLOCKS,), 0, 8) == 0
    forced = jax.random.randint(prng_seed_handles[2], (), 0, SEQ_BLOCKS)
    row_index = jnp.arange(SEQ_BLOCKS)
    listed = jnp.where(row_index == forced, RESETS_DEV, jnp.where(active, listed, 0))

    def pick_row(row_key):
        return jax.random.permutation(row_key, TOK_DEV)[:RESETS_DEV]
    picks = jax.vmap(pick_row)(jax.random.split(prng_seed_handles[3], SEQ_BLOCKS))
    slots = jnp.arange(RESETS_DEV)[None, :]
    chosen = jnp.where(slots < listed[:, None], picks, TOK_DEV)
    return jnp.sort(chosen, axis=1).astype(jnp.int32)


def levels(key, shape, pieces, least, high):
    gain, own = 1.0, jax.random.fold_in(key, 6)
    for axis_at, blocks in pieces:
        draws = jnp.exp(jax.random.uniform(jax.random.fold_in(own, axis_at), (blocks,), jnp.float32, least / len(pieces), high / len(pieces)))
        gain = gain * jnp.repeat(draws, shape[axis_at] // blocks).reshape([-1 if axis == axis_at else 1 for axis in range(len(shape))])
    return gain


def bell_draw(own_key, shape, deviation, bound, shards=(), kind=jnp.bfloat16):
    gain = levels(own_key, shape, shards, -0.22, 0.18) if shards else 1.0
    entries = jax.random.normal(own_key, shape, jnp.float32) * deviation * gain
    return jnp.minimum(jnp.maximum(entries, -bound), bound).astype(kind)


def setup_inputs(seed: int = 0) -> dict:
    seeds = jax.random.split(jax.random.key(seed), 8)
    return {
        "mixer_input": bell_draw(seeds[0], (JOINED_POSITIONS, HEADS * HEAD_DIM), 1.0, 6.0, ((0, 32), (1, 8))),
        "write_rows": bell_draw(seeds[1], (JOINED_POSITIONS, STATE), 0.3, 1.796875, ((0, 256),)),
        "read_rows": bell_draw(seeds[2], (JOINED_POSITIONS, STATE), 0.3, 1.796875, ((0, 256),)),
        "log_decay": draw_log_decay(jax.random.fold_in(seeds[7], 71), 0),
        "skip_gain": jnp.clip(1.0 + 0.15 * jax.random.normal(seeds[4], (HEADS,), jnp.float32), 0.25, 1.75),
        "reset_offsets": draw_reset_offsets(jax.random.fold_in(seeds[7], 71), 0),
        "grad_out": bell_draw(seeds[6], (JOINED_POSITIONS, HEADS * HEAD_DIM), 1.0, 6.0, ((0, 32), (1, 8))),
    }


def span_update(carry_state, inputs, skip_gain):
    feature_part, write_part, read_part, log_part, reset_part = inputs
    span_len = reset_part.shape[0]
    cum_log = jnp.cumsum(log_part, axis=1)
    reset_count = jnp.cumsum(reset_part)
    input_gain = jnp.sqrt(-jnp.expm1(2.0 * log_part))
    positions = jnp.arange(span_len)
    allowed = (positions[:, None] >= positions[None, :]) & (reset_count[:, None] == reset_count[None, :])
    spread = cum_log[:, :, None] - cum_log[:, None, :]
    decay_matrix = jnp.exp(jnp.where(allowed[None], spread, -1e+30))
    scores = jnp.dot(read_part, write_part.T, precision=lax.Precision.HIGHEST)
    weights = decay_matrix * scores[None] * input_gain[:, None, :]
    result = jnp.einsum('hts,shp->thp', weights, feature_part, precision=lax.Precision.HIGHEST)
    entry_decay = jnp.exp(cum_log) * (reset_count == 0)[None, :]
    carried = jnp.einsum('tn,hnp->thp', read_part, carry_state, precision=lax.Precision.HIGHEST)
    result = result + carried * entry_decay.T[:, :, None] + skip_gain[None, :, None] * feature_part
    tail_weight = jnp.exp(cum_log[:, -1:] - cum_log) * (reset_count == reset_count[-1])[None, :] * input_gain
    block_decay = jnp.exp(cum_log[:, -1]) * (reset_count[-1] == 0)
    fresh_state = jnp.einsum('sn,shp->hnp', write_part, feature_part * tail_weight.T[:, :, None], precision=lax.Precision.HIGHEST)
    return (block_decay[:, None, None] * carry_state + fresh_state, result)

def forward_all(feature_full, write_full, read_full, log_decay, resets, skip_gain):
    spans = JOINED_POSITIONS // SPAN
    feature_blocks = feature_full.reshape(spans, SPAN, HEADS, HEAD_DIM)
    write_blocks = write_full.reshape(spans, SPAN, STATE)
    read_blocks = read_full.reshape(spans, SPAN, STATE)
    log_blocks = log_decay.reshape(HEADS, spans, SPAN).transpose(1, 0, 2)
    reset_blocks = resets.reshape(spans, SPAN)

    def advance(carry_state, inputs):
        return span_update(carry_state, inputs, skip_gain)
    initial = jnp.zeros((HEADS, STATE, HEAD_DIM), jnp.float32)
    end_state, outputs = lax.scan(jax.checkpoint(advance), initial, (feature_blocks, write_blocks, read_blocks, log_blocks, reset_blocks))
    return outputs.reshape(JOINED_POSITIONS, HEADS, HEAD_DIM)

def reference(mixer_input, write_rows, read_rows, log_decay, skip_gain, reset_offsets, grad_out):
    row_count = reset_offsets.shape[0]
    block_start = jnp.arange(row_count, dtype=jnp.int32)[:, None] * TOK_DEV
    spots = jnp.where(reset_offsets < TOK_DEV, reset_offsets + block_start, JOINED_POSITIONS).reshape(-1).astype(jnp.int32)
    resets = jnp.zeros((JOINED_POSITIONS,), jnp.float32).at[spots].set(1.0, mode='drop')

    def mixer(feature_full, write_full, read_full):
        return forward_all(feature_full, write_full, read_full, log_decay, resets, skip_gain)
    feature_full = mixer_input.astype(jnp.float32).reshape(JOINED_POSITIONS, HEADS, HEAD_DIM)
    outputs, pullback = jax.vjp(mixer, feature_full, write_rows.astype(jnp.float32), read_rows.astype(jnp.float32))
    grad_feature, grad_write, grad_read = pullback(grad_out.astype(jnp.float32).reshape(JOINED_POSITIONS, HEADS, HEAD_DIM))
    return (grad_feature.reshape(JOINED_POSITIONS, HEADS * HEAD_DIM).astype(jnp.bfloat16), grad_write, grad_read)
```

```python
import functools

import jax
import jax.numpy as jnp
import numpy as np
from jax import lax
from jax.experimental import pallas as pl
from jax.experimental.pallas import tpu as pltpu
from jax.sharding import PartitionSpec as P

F32 = jnp.float32
BF16 = jnp.bfloat16
TOK = 2048
HEADS = 10
PAD = 16
WIDTH = 640
STATE = 128
Q = 128
CHUNKS = TOK // Q
BLOCK = 256
BLOCKS = TOK // BLOCK
VMEM = 28 * 1024 * 1024
LOG2E = 1.4426950408889634
NEG = -1e30


def spread(first):
    out = np.zeros((STATE, WIDTH), np.float32)
    for j in range(WIDTH):
        out[first + j // 64, j] = 1.0
        out[first + PAD + j // 64, j] = 1.0
    return out


SPREAD_D = np.concatenate([spread(0), spread(32)], axis=1)
SPREAD_C = np.concatenate([spread(64), spread(96)], axis=1)
SPREAD_F = spread(0)


def nt(a, b):
    return lax.dot_general(a, b, (((1,), (1,)), ((), ())), preferred_element_type=F32)


def tn(a, b):
    return lax.dot_general(a, b, (((0,), (0,)), ((), ())), preferred_element_type=F32)


def nn(a, b):
    return lax.dot_general(a, b, (((1,), (0,)), ((), ())), preferred_element_type=F32)


WHOLE = pl.BlockSpec(memory_space=pltpu.VMEM)
SCALARS = pl.BlockSpec(memory_space=pltpu.SMEM)
FAR = pl.BlockSpec(memory_space=pltpu.HBM)


def far(*arrays):
    return [pltpu.with_memory_space_constraint(a, pltpu.HBM) for a in arrays]


def far_out(shape, dtype):
    return pltpu.HBM(shape, dtype)


def block_copy(src, dst, sem, which, i, rows=BLOCK):
    r = pl.ds(pl.multiple_of(i * rows, rows), rows)
    return pltpu.make_async_copy(src.at[r], dst.at[r], sem.at[which, i])


def options():
    return pltpu.CompilerParams(vmem_limit_bytes=VMEM)


def cost(flops, moved):
    return pl.CostEstimate(flops=int(flops), bytes_accessed=int(moved), transcendentals=0)


def starts_until(off, t):
    count = jnp.where(t >= off[0, 0], 1, 0)
    for i in range(1, 4):
        count = count + jnp.where(t >= off[0, i], 1, 0)
    return count


def decay_part(off, l_ref, gain_ref, lg_ref, lrow_ref, lshift_ref, sc_ref, dec_ref):
    lane = lax.broadcasted_iota(jnp.int32, (PAD, Q), 1)
    rev = [None] * CHUNKS
    fwd = [None] * CHUNKS
    for c in range(CHUNKS):
        x = l_ref[:, c * Q : (c + 1) * Q]
        y, z = x, x
        for k in (1, 2, 4, 8, 16, 32, 64):
            y = y + jnp.where(lane >= k, pltpu.roll(y, k, 1), 0.0)
            z = z + jnp.where(lane < Q - k, pltpu.roll(z, Q - k, 1), 0.0)
        fwd[c] = y
        rev[c] = jnp.where(lane < Q - 1, pltpu.roll(z, Q - 1, 1), 0.0)
    ends = [fwd[c][:, Q - 1 : Q] for c in range(CHUNKS)]
    before = [jnp.zeros((PAD, 1), F32)]
    for c in range(CHUNKS):
        before.append(before[-1] + ends[c])
    after = [jnp.zeros((PAD, 1), F32)]
    for c in range(CHUNKS - 1, 0, -1):
        after.append(after[-1] + ends[c])
    after = after[::-1]
    last_count = starts_until(off, jnp.int32(TOK - 1))
    decs = jnp.zeros((PAD, Q), F32)
    for c in range(CHUNKS):
        t = lane + c * Q
        seg = starts_until(off, t)
        seg_b = starts_until(off, jnp.int32(c * Q - 1))
        seg_e = starts_until(off, jnp.int32(c * Q + Q - 1))
        gain = gain_ref[:, c * Q : (c + 1) * Q]
        tail_d = jnp.where(seg == last_count, jnp.exp2(rev[c] + after[c]) * gain, 0.0)
        entry_d = jnp.where(seg == 0, jnp.exp2(fwd[c] + before[c]), 0.0)
        tail_c = jnp.where(seg == seg_e, jnp.exp2(rev[c]) * gain, 0.0)
        entry_c = jnp.where(seg == seg_b, jnp.exp2(fwd[c]), 0.0)
        rows = []
        for v in (tail_d, entry_d, tail_c, entry_c):
            hi = v.astype(BF16).astype(F32)
            rows += [hi, v - hi]
        sc_ref[c * Q : (c + 1) * Q, :] = jnp.concatenate(rows, axis=0).T.astype(BF16)
        lrow_ref[:, c * Q : (c + 1) * Q] = fwd[c]
        lshift_ref[:, c * Q : (c + 1) * Q] = fwd[c] - lg_ref[:, c * Q : (c + 1) * Q]
        keep_c = jnp.where(seg_b == seg_e, 1.0, 0.0)
        decs = jnp.where(lane == c, jnp.exp2(ends[c]) * keep_c, decs)
        keep_after = jnp.where(seg_e == last_count, 1.0, 0.0)
        decs = jnp.where(lane == 32 + c, jnp.exp2(after[c]) * keep_after, decs)
    keep = jnp.where(last_count == 0, 1.0, 0.0)
    decs = jnp.where(lane == CHUNKS, jnp.exp2(before[CHUNKS]) * keep, decs)
    hi = decs.astype(BF16).astype(F32)
    full = jnp.concatenate([hi, decs - hi, jnp.zeros((Q - 2 * PAD, Q), F32)], axis=0)
    dec_ref[...] = full.T.astype(BF16)


def prepare_kernel(
    off, l_ref, gain_ref, lg_ref, x_hbm, g_hbm, sp_ref,
    lrow_ref, lshift_ref, sc_ref, dec_ref, xt_hbm, ge_hbm, x_ref, g_ref, in_sem, out_sem,
):
    for i in range(BLOCKS):
        block_copy(x_hbm, x_ref, in_sem, 0, i).start()
        block_copy(g_hbm, g_ref, in_sem, 1, i).start()
    decay_part(off, l_ref, gain_ref, lg_ref, lrow_ref, lshift_ref, sc_ref, dec_ref)

    @pl.loop(0, BLOCKS)
    def _(i):
        block_copy(x_hbm, x_ref, in_sem, 0, i).wait()
        block_copy(g_hbm, g_ref, in_sem, 1, i).wait()
        r = pl.ds(pl.multiple_of(i * BLOCK, BLOCK), BLOCK)
        s = nn(sc_ref[r, :], sp_ref[...])
        x_ref[r, :] = (x_ref[r, :].astype(F32) * s[:, :WIDTH]).astype(BF16)
        g_ref[r, :] = (g_ref[r, :].astype(F32) * s[:, WIDTH:]).astype(BF16)
        block_copy(x_ref, xt_hbm, out_sem, 0, i).start()
        block_copy(g_ref, ge_hbm, out_sem, 1, i).start()

    for i in range(BLOCKS):
        block_copy(x_ref, xt_hbm, out_sem, 0, i).wait()
        block_copy(g_ref, ge_hbm, out_sem, 1, i).wait()


def prepare_call(off, log_decay, x, g, sp):
    l = jnp.pad(log_decay, ((0, PAD - HEADS), (0, 0)), constant_values=-1.0)
    square = -jnp.expm1(2.0 * l)
    return pl.pallas_call(
        prepare_kernel,
        out_shape=(
            jax.ShapeDtypeStruct((PAD, TOK), F32),
            jax.ShapeDtypeStruct((PAD, TOK), F32),
            far_out((TOK, STATE), BF16),
            jax.ShapeDtypeStruct((STATE, STATE), BF16),
            far_out((TOK, WIDTH), BF16),
            far_out((TOK, WIDTH), BF16),
        ),
        in_specs=[SCALARS, WHOLE, WHOLE, WHOLE, FAR, FAR, WHOLE],
        out_specs=(WHOLE,) * 4 + (FAR,) * 2,
        scratch_shapes=[pltpu.VMEM((TOK, WIDTH), BF16)] * 2 + [pltpu.SemaphoreType.DMA((2, BLOCKS))] * 2,
        compiler_params=options(),
        cost_estimate=cost(4e9, 16e6),
        name="prepare",
    )(off, l * LOG2E, jnp.sqrt(square), 0.5 * jnp.log2(square), *far(x, g), sp)


def state_kernel(
    place, m0, m1, m2, m3, o0, o1, o2, o3, xt_hbm, ge_hbm, dec_ref, out_ref, bc_hbm,
    xt_ref, ge_ref, bc_ref, in_sem, out_sem,
):
    rows = TOK // 4
    for i in range(4):
        block_copy(xt_hbm, xt_ref, in_sem, 0, i, rows).start()
        block_copy(ge_hbm, ge_ref, in_sem, 1, i, rows).start()
    core, y = place[0], place[1]
    for k, (m, o) in enumerate(((m0, o0), (m1, o1), (m2, o2), (m3, o3))):
        pair = lax.rem(y + 4 - k, 4) * 2
        bc_ref[pl.ds(pl.multiple_of((pair + core) * BLOCK, BLOCK), BLOCK), :] = m[...]
        bc_ref[pl.ds(pl.multiple_of((pair + 1 - core) * BLOCK, BLOCK), BLOCK), :] = o[...]
    save = pltpu.make_async_copy(bc_ref, bc_hbm, out_sem)
    save.start()
    for i in range(4):
        block_copy(xt_hbm, xt_ref, in_sem, 0, i, rows).wait()
        block_copy(ge_hbm, ge_ref, in_sem, 1, i, rows).wait()
    s = nn(bc_ref[:, :STATE].T, xt_ref[...])
    out_ref[:16, :, :WIDTH] = s.reshape(16, 8, WIDTH).astype(BF16)
    t = nn(bc_ref[:, STATE:].T, ge_ref[...])
    out_ref[16:, :, :WIDTH] = t.reshape(16, 8, WIDTH).astype(BF16)
    row = dec_ref[CHUNKS : CHUNKS + 1, :].astype(F32)
    out_ref[:, :, WIDTH:] = jnp.broadcast_to(row[None], (32, 8, STATE)).astype(BF16)
    save.wait()


def state_call(place, pieces, xt, ge, dec):
    return pl.pallas_call(
        state_kernel,
        out_shape=(jax.ShapeDtypeStruct((32, 8, WIDTH + STATE), BF16), far_out((TOK, 2 * STATE), BF16)),
        in_specs=[SCALARS] + [WHOLE] * 8 + [FAR, FAR, WHOLE],
        out_specs=(WHOLE, FAR),
        scratch_shapes=[pltpu.VMEM((TOK, WIDTH), BF16)] * 2
        + [pltpu.VMEM((TOK, 2 * STATE), BF16), pltpu.SemaphoreType.DMA((2, 4)), pltpu.SemaphoreType.DMA],
        compiler_params=options(),
        cost_estimate=cost(7e8, 6.5e6),
        name="states",
    )(place, *pieces, *far(xt, ge), dec)


def scan_kernel(me, in_ref, sp_ref, out_ref, d_ref):
    rows = in_ref[:, :, WIDTH:].astype(F32).reshape(256, STATE).astype(BF16)
    d_ref[...] = nn(rows, sp_ref[...]).reshape(32, 8, WIDTH)
    backward = me[0] >= 16

    def one(k, state):
        b = jnp.where(backward, 31 - k, k)
        out_ref[b] = state.astype(BF16)
        return d_ref[b] * state + in_ref[b, :, :WIDTH].astype(F32)

    lax.fori_loop(0, 32, one, jnp.zeros((8, WIDTH), F32), unroll=True)


def scan_call(me, part, sp):
    vm = pl.BlockSpec(memory_space=pltpu.VMEM)
    return pl.pallas_call(
        scan_kernel,
        out_shape=jax.ShapeDtypeStruct((32, 8, WIDTH), BF16),
        in_specs=[pl.BlockSpec(memory_space=pltpu.SMEM), vm, vm],
        out_specs=vm,
        scratch_shapes=[pltpu.VMEM((32, 8, WIDTH), F32)],
        compiler_params=pltpu.CompilerParams(vmem_limit_bytes=VMEM),
        name="scan",
    )(me, part, sp)


def within_kernel(
    off, x_hbm, g_hbm, bc_hbm, lrow_ref, lshift_ref, skip_ref, gx_hbm, z_hbm,
    x_ref, g_ref, bc_ref, gx_ref, z_ref, in_sem, out_sem,
):
    for i in range(BLOCKS):
        block_copy(bc_hbm, bc_ref, in_sem, 2, i).start()
        block_copy(x_hbm, x_ref, in_sem, 0, i).start()
        block_copy(g_hbm, g_ref, in_sem, 1, i).start()
    si = lax.broadcasted_iota(jnp.int32, (Q, Q), 0)
    ti = lax.broadcasted_iota(jnp.int32, (Q, Q), 1)
    even = lax.broadcasted_iota(jnp.int32, (Q, Q), 1) < 64
    odd = jnp.logical_not(even)
    zero = jnp.zeros((Q, Q), BF16)

    @pl.loop(0, BLOCKS)
    def _(step):
        block_copy(bc_hbm, bc_ref, in_sem, 2, step).wait()
        block_copy(x_hbm, x_ref, in_sem, 0, step).wait()
        block_copy(g_hbm, g_ref, in_sem, 1, step).wait()
        for sub in range(BLOCK // Q):
            base = pl.multiple_of(step * BLOCK + sub * Q, Q)
            r = pl.ds(base, Q)
            same = starts_until(off, si + base) == starts_until(off, ti + base)
            bias = jnp.where((ti >= si) & same, 0.0, NEG)
            lt = lrow_ref[:, r]
            ls = lshift_ref[:, r].T
            scores = nt(bc_ref[r, :STATE], bc_ref[r, STATE:])
            z = jnp.zeros((Q, Q), F32)
            for p in range(HEADS // 2):
                w = slice(p * Q, (p + 1) * Q)
                x = x_ref[r, w]
                g = g_ref[r, w]
                e = nt(jnp.concatenate([jnp.where(even, x, zero), jnp.where(odd, x, zero)], axis=0), g)
                h = 2 * p
                ma = jnp.exp2(lt[h : h + 1, :] - ls[:, h : h + 1] + bias)
                mb = jnp.exp2(lt[h + 1 : h + 2, :] - ls[:, h + 1 : h + 2] + bias)
                z = z + (ma * e[:Q] + mb * e[Q:])
                weights = jnp.concatenate([(ma * scores).astype(BF16), (mb * scores).astype(BF16)], axis=1)
                both = jnp.concatenate([jnp.where(even, g, zero), jnp.where(odd, g, zero)], axis=0)
                gx_ref[r, w] = (nn(weights, both) + g.astype(F32) * skip_ref[:, w]).astype(BF16)
            z_ref[r, :] = z.astype(BF16)
        block_copy(gx_ref, gx_hbm, out_sem, 0, step).start()
        block_copy(z_ref, z_hbm, out_sem, 1, step).start()

    for i in range(BLOCKS):
        block_copy(gx_ref, gx_hbm, out_sem, 0, i).wait()
        block_copy(z_ref, z_hbm, out_sem, 1, i).wait()


def within_call(off, x, g, bc, lrow, lshift, skip):
    return pl.pallas_call(
        within_kernel,
        out_shape=(far_out((TOK, WIDTH), BF16), far_out((TOK, STATE), BF16)),
        in_specs=[SCALARS, FAR, FAR, FAR, WHOLE, WHOLE, WHOLE],
        out_specs=(FAR, FAR),
        scratch_shapes=[
            pltpu.VMEM((TOK, WIDTH), BF16),
            pltpu.VMEM((TOK, WIDTH), BF16),
            pltpu.VMEM((TOK, 2 * STATE), BF16),
            pltpu.VMEM((TOK, WIDTH), BF16),
            pltpu.VMEM((TOK, STATE), BF16),
            pltpu.SemaphoreType.DMA((3, BLOCKS)),
            pltpu.SemaphoreType.DMA((2, BLOCKS)),
        ],
        compiler_params=options(),
        cost_estimate=cost(4e9, 16e6),
        name="within_chunks",
    )(off, *far(x, g, bc), lrow, lshift, skip)


def chain_kernel(
    x_hbm, g_hbm, bc_hbm, sc_hbm, z_hbm, dec_ref, sp_ref, spf_ref, gc_hbm, gb_hbm, tst_hbm,
    x_ref, g_ref, bc_ref, sc_ref, z_ref, gc_ref, gb_ref, tst_ref, s_ref, t_ref, d_ref, in_sem, out_sem,
):
    loads = ((sc_hbm, sc_ref), (x_hbm, x_ref), (g_hbm, g_ref), (bc_hbm, bc_ref), (z_hbm, z_ref))
    for i in range(BLOCKS // 2):
        for j in (i, BLOCKS - 1 - i):
            for n, (src, dst) in enumerate(loads):
                block_copy(src, dst, in_sem, n, j).start()
    s_ref[...] = jnp.zeros_like(s_ref)
    t_ref[...] = jnp.zeros_like(t_ref)
    d_ref[...] = nn(dec_ref[:CHUNKS, :], spf_ref[...])
    per = BLOCK // Q

    @pl.loop(0, BLOCKS)
    def _(step):
        @pl.when(step < BLOCKS // 2)
        def _():
            for j in (step, BLOCKS - 1 - step):
                for n, (src, dst) in enumerate(loads):
                    block_copy(src, dst, in_sem, n, j).wait()
                for sub in range(per):
                    r = pl.ds(pl.multiple_of(j * BLOCK + sub * Q, Q), Q)
                    s = nn(sc_ref[r, :], sp_ref[...])
                    x_ref[r, :] = (x_ref[r, :].astype(F32) * s[:, :WIDTH]).astype(BF16)
                    g_ref[r, :] = (g_ref[r, :].astype(F32) * s[:, WIDTH:]).astype(BF16)

        back = BLOCKS - 1 - step
        for sub in range(per):
            c = step * per + sub
            r = pl.ds(pl.multiple_of(c * Q, Q), Q)
            state = s_ref[...]
            b = bc_ref[r, :STATE]
            gc_ref[r, :] = tn(z_ref[r, :], b) + nt(g_ref[r, :], state.astype(BF16))
            s_ref[...] = d_ref[pl.ds(c, 1), :] * state + tn(b, x_ref[r, :])
            c = back * per + per - 1 - sub
            r = pl.ds(pl.multiple_of(c * Q, Q), Q)
            state = t_ref[...]
            low = state.astype(BF16)
            tst_ref[c] = low
            q = bc_ref[r, STATE:]
            gb_ref[r, :] = nn(z_ref[r, :], q) + nt(x_ref[r, :], low)
            t_ref[...] = d_ref[pl.ds(c, 1), :] * state + tn(q, g_ref[r, :])
        block_copy(gc_ref, gc_hbm, out_sem, 0, step).start()
        block_copy(gb_ref, gb_hbm, out_sem, 1, back).start()
        block_copy(tst_ref, tst_hbm, out_sem, 2, back, per).start()

    for i in range(BLOCKS):
        block_copy(gc_ref, gc_hbm, out_sem, 0, i).wait()
        block_copy(gb_ref, gb_hbm, out_sem, 1, i).wait()
        block_copy(tst_ref, tst_hbm, out_sem, 2, i, per).wait()


def chain_call(x, g, bc, sc, z, dec, sp, spf):
    return pl.pallas_call(
        chain_kernel,
        out_shape=(
            far_out((TOK, STATE), F32),
            far_out((TOK, STATE), F32),
            far_out((CHUNKS, STATE, WIDTH), BF16),
        ),
        in_specs=[FAR] * 5 + [WHOLE] * 3,
        out_specs=(FAR,) * 3,
        scratch_shapes=[
            pltpu.VMEM((TOK, WIDTH), BF16),
            pltpu.VMEM((TOK, WIDTH), BF16),
            pltpu.VMEM((TOK, 2 * STATE), BF16),
            pltpu.VMEM((TOK, STATE), BF16),
            pltpu.VMEM((TOK, STATE), BF16),
            pltpu.VMEM((TOK, STATE), F32),
            pltpu.VMEM((TOK, STATE), F32),
            pltpu.VMEM((CHUNKS, STATE, WIDTH), BF16),
            pltpu.VMEM((STATE, WIDTH), F32),
            pltpu.VMEM((STATE, WIDTH), F32),
            pltpu.VMEM((CHUNKS, WIDTH), F32),
            pltpu.SemaphoreType.DMA((5, BLOCKS)),
            pltpu.SemaphoreType.DMA((3, BLOCKS)),
        ],
        compiler_params=options(),
        cost_estimate=cost(4e9, 16e6),
        name="chunk_chain",
    )(*far(x, g, bc, sc, z), dec, sp, spf)


def carry_kernel(
    place, xt_hbm, ge_hbm, gb_hbm, gc_hbm, st_ref, keep_ref, send_ref, xt_ref, ge_ref, gb_ref, gc_ref, in_sem
):
    core = place[0]
    loads = ((xt_hbm, xt_ref), (ge_hbm, ge_ref), (gb_hbm, gb_ref), (gc_hbm, gc_ref))
    for i in range(BLOCKS):
        for n, (src, dst) in enumerate(loads):
            block_copy(src, dst, in_sem, n, i).start()
    s = st_ref[:STATE, :]
    t = st_ref[STATE:, :]
    for i in range(4):
        for n, (src, dst) in enumerate(loads):
            block_copy(src, dst, in_sem, n, 2 * i).wait()
            block_copy(src, dst, in_sem, n, 2 * i + 1).wait()
        r = pl.ds(pl.multiple_of((2 * i + core) * BLOCK, BLOCK), BLOCK)
        keep_ref[i, :, :STATE] = gb_ref[r, :] + nt(xt_ref[r, :], t)
        keep_ref[i, :, STATE:] = gc_ref[r, :] + nt(ge_ref[r, :], s)
        r = pl.ds(pl.multiple_of((2 * i + 1 - core) * BLOCK, BLOCK), BLOCK)
        send_ref[i, :, :STATE] = (gb_ref[r, :] + nt(xt_ref[r, :], t)).astype(BF16)
        send_ref[i, :, STATE:] = (gc_ref[r, :] + nt(ge_ref[r, :], s)).astype(BF16)


def carry_call(place, xt, ge, gb, gc, st):
    return pl.pallas_call(
        carry_kernel,
        out_shape=(
            jax.ShapeDtypeStruct((4, BLOCK, 2 * STATE), F32),
            jax.ShapeDtypeStruct((4, BLOCK, 2 * STATE), BF16),
        ),
        in_specs=[SCALARS] + [FAR] * 4 + [WHOLE],
        out_specs=(WHOLE, WHOLE),
        scratch_shapes=[
            pltpu.VMEM((TOK, WIDTH), BF16),
            pltpu.VMEM((TOK, WIDTH), BF16),
            pltpu.VMEM((TOK, STATE), F32),
            pltpu.VMEM((TOK, STATE), F32),
            pltpu.SemaphoreType.DMA((4, BLOCKS)),
        ],
        compiler_params=options(),
        cost_estimate=cost(7e8, 9e6),
        name="carry",
    )(place, *far(xt, ge, gb, gc), st)


def input_kernel(
    gx_hbm, tst_hbm, bc_hbm, sc_hbm, st_ref, sp_ref, dec_ref, spf_ref, out_hbm,
    gx_ref, tst_ref, bc_ref, sc_ref, d_ref, in_sem, out_sem,
):
    per = BLOCK // Q
    loads = ((gx_hbm, gx_ref, BLOCK), (tst_hbm, tst_ref, per), (bc_hbm, bc_ref, BLOCK), (sc_hbm, sc_ref, BLOCK))
    for i in range(BLOCKS):
        for n, (src, dst, rows) in enumerate(loads):
            block_copy(src, dst, in_sem, n, i, rows).start()
    d_ref[...] = nn(dec_ref[32 : 32 + CHUNKS, :], spf_ref[...])

    @pl.loop(0, BLOCKS)
    def _(step):
        for n, (src, dst, rows) in enumerate(loads):
            block_copy(src, dst, in_sem, n, step, rows).wait()
        for sub in range(per):
            c = step * per + sub
            r = pl.ds(pl.multiple_of(c * Q, Q), Q)
            full = tst_ref[c].astype(F32) + d_ref[pl.ds(c, 1), :] * st_ref[STATE:, :].astype(F32)
            scale = nn(sc_ref[r, :], sp_ref[:, :WIDTH])
            gx_ref[r, :] = (gx_ref[r, :].astype(F32) + scale * nn(bc_ref[r, :STATE], full.astype(BF16))).astype(BF16)
        block_copy(gx_ref, out_hbm, out_sem, 0, step).start()

    for i in range(BLOCKS):
        block_copy(gx_ref, out_hbm, out_sem, 0, i).wait()


def input_call(gx, tst, st, bc, sc, sp, dec, spf):
    return pl.pallas_call(
        input_kernel,
        out_shape=jax.ShapeDtypeStruct((TOK, WIDTH), BF16),
        in_specs=[FAR] * 4 + [WHOLE] * 4,
        out_specs=FAR,
        scratch_shapes=[
            pltpu.VMEM((TOK, WIDTH), BF16),
            pltpu.VMEM((CHUNKS, STATE, WIDTH), BF16),
            pltpu.VMEM((TOK, 2 * STATE), BF16),
            pltpu.VMEM((TOK, STATE), BF16),
            pltpu.VMEM((CHUNKS, WIDTH), F32),
            pltpu.SemaphoreType.DMA((4, BLOCKS)),
            pltpu.SemaphoreType.DMA((1, BLOCKS)),
        ],
        compiler_params=options(),
        cost_estimate=cost(2e9, 12e6),
        name="input_gradient",
    )(*far(gx, tst, bc, sc), st, sp, dec, spf)


def join_kernel(a_ref, b_ref, out_ref):
    out_ref[:, :STATE] = a_ref[...]
    out_ref[:, STATE:] = b_ref[...]


def join_call(a, b):
    return pl.pallas_call(
        join_kernel, out_shape=jax.ShapeDtypeStruct((BLOCK, 2 * STATE), BF16), compiler_params=options(), name="join"
    )(a, b)


def pair_kernel(place, keep_ref, got_ref, o0, o1, o2, o3):
    y = place[1]
    for k, o in enumerate((o0, o1, o2, o3)):
        j = lax.rem(y + k, 4)
        o[...] = (keep_ref[j] + got_ref[j].astype(F32)).astype(o.dtype)


def pair_call(place, keep, got):
    return pl.pallas_call(
        pair_kernel,
        out_shape=(jax.ShapeDtypeStruct((BLOCK, 2 * STATE), F32),)
        + (jax.ShapeDtypeStruct((BLOCK, 2 * STATE), BF16),) * 3,
        in_specs=[SCALARS, WHOLE, WHOLE],
        out_specs=(WHOLE,) * 4,
        compiler_params=options(),
        name="pair_sums",
    )(place, keep, got)


def total_kernel(a_ref, b_ref, c_ref, d_ref, w_ref, r_ref):
    t = a_ref[...] + b_ref[...].astype(F32) + c_ref[...].astype(F32) + d_ref[...].astype(F32)
    w_ref[...] = t[:, :STATE]
    r_ref[...] = t[:, STATE:]


def total_call(*parts):
    return pl.pallas_call(
        total_kernel,
        out_shape=(jax.ShapeDtypeStruct((BLOCK, STATE), F32),) * 2,
        compiler_params=options(),
        name="totals",
    )(*parts)


def along_y(k):
    return [(i, (i + 2 * k) % 8) for i in range(8)]


SWAP = [(i, i ^ 1) for i in range(8)]


def shards(mixer_input, write_rows, read_rows, log_decay, skip_gain, reset_offsets, grad_out):
    spot = lax.axis_index("head").astype(jnp.int32)
    core, y = spot & 1, spot >> 1
    place = jnp.stack([core, y])
    me = lax.axis_index("seq").astype(jnp.int32).reshape(1)
    spread_d, spread_c, spread_f = (jnp.asarray(a, BF16) for a in (SPREAD_D, SPREAD_C, SPREAD_F))
    own = join_call(write_rows, read_rows)
    mine = [own] + [lax.ppermute(own, "head", along_y(k)) for k in (1, 2, 3)]
    lrow, lshift, sc, dec, xt, ge = prepare_call(reset_offsets, log_decay, mixer_input, grad_out, spread_d)
    *mine, xt, ge = lax.optimization_barrier((*mine, xt, ge))
    other = [lax.ppermute(a, "head", SWAP) for a in mine]
    payload, bc = state_call(place, mine + other, xt, ge, dec)
    parts = lax.all_to_all(payload, "seq", 0, 0, tiled=True)
    skip = jnp.repeat(skip_gain, 64)[None, :]
    gx, z = within_call(reset_offsets, mixer_input, grad_out, bc, lrow, lshift, skip)
    parts, gx, z = lax.optimization_barrier((parts, gx, z))
    entering = scan_call(me, parts, spread_f)
    st = lax.all_to_all(entering, "seq", 0, 0, tiled=True).reshape(2 * STATE, WIDTH)
    gc, gb, tst = chain_call(mixer_input, grad_out, bc, sc, z, dec, spread_c, spread_f)
    keep, send = carry_call(place, xt, ge, gb, gc, st)
    total, *leaving = pair_call(place, keep, lax.ppermute(send, "head", SWAP))
    arrived = [lax.ppermute(a, "head", along_y(k)) for k, a in zip((1, 2, 3), leaving)]
    grad_input = input_call(gx, tst, st, bc, sc, spread_c, dec, spread_f)
    return (grad_input, *total_call(total, *arrived))


def solution(mesh):
    in_specs = (
        P("seq", "head"),
        P(("seq", "head"), None),
        P(("seq", "head"), None),
        P("head", "seq"),
        P("head"),
        P("seq", None),
        P("seq", "head"),
    )
    out_specs = (P("seq", "head"), P(("seq", "head"), None), P(("seq", "head"), None))
    return jax.shard_map(shards, mesh=mesh, in_specs=in_specs, out_specs=out_specs, check_vma=False)
```

```python
import functools

import jax
import jax.numpy as jnp
import numpy as np
from jax import lax
from jax.experimental import pallas as pl
from jax.experimental.pallas import tpu as pltpu
from jax.sharding import PartitionSpec as P

F32 = jnp.float32
BF16 = jnp.bfloat16
TOK = 2048
HEADS = 10
PAD = 16
WIDTH = 640
STATE = 128
Q = 128
CHUNKS = TOK // Q
BLOCK = 256
BLOCKS = TOK // BLOCK
VMEM = 28 * 1024 * 1024
NEG = -1e30
AHEAD = 2


def spread(first):
    out = np.zeros((STATE, WIDTH), np.float32)
    for j in range(WIDTH):
        out[first + j // 64, j] = 1.0
        out[first + PAD + j // 64, j] = 1.0
    return out


SPREAD_D = np.concatenate([spread(0), spread(32)], axis=1)
SPREAD_C = np.concatenate([spread(64), spread(96)], axis=1)
SPREAD_F = spread(0)
SUMS = np.concatenate([np.triu(np.ones((Q, Q))), np.tril(np.ones((Q, Q)), -1)], axis=1).astype(np.float32)


def nt(a, b):
    return lax.dot_general(a, b, (((1,), (1,)), ((), ())), preferred_element_type=F32)


def tn(a, b):
    return lax.dot_general(a, b, (((0,), (0,)), ((), ())), preferred_element_type=F32)


def nn(a, b):
    return lax.dot_general(a, b, (((1,), (0,)), ((), ())), preferred_element_type=F32)


WHOLE = pl.BlockSpec(memory_space=pltpu.VMEM)
SCALARS = pl.BlockSpec(memory_space=pltpu.SMEM)
FAR = pl.BlockSpec(memory_space=pltpu.HBM)


def far(*arrays):
    return [pltpu.with_memory_space_constraint(a, pltpu.HBM) for a in arrays]


def kept(shape, dtype):
    return pltpu.VMEM(shape, dtype)


def held(*arrays):
    return [pltpu.with_memory_space_constraint(a, pltpu.VMEM) for a in arrays]


def far_out(shape, dtype):
    return pltpu.HBM(shape, dtype)


def block_copy(src, dst, sem, which, i, rows=BLOCK):
    r = pl.ds(pl.multiple_of(i * rows, rows), rows)
    return pltpu.make_async_copy(src.at[r], dst.at[r], sem.at[which, i])


def options():
    return pltpu.CompilerParams(vmem_limit_bytes=VMEM)


def cost(flops, moved):
    return pl.CostEstimate(flops=int(flops), bytes_accessed=int(moved), transcendentals=0)


def starts_until(off, t):
    count = jnp.where(t >= off[0, 0], 1, 0)
    for i in range(1, 4):
        count = count + jnp.where(t >= off[0, i], 1, 0)
    return count


def minus_expm1(y):
    series = 1.0 + y * (1.0 / 10)
    for n in range(9, 1, -1):
        series = 1.0 + y * (1.0 / n) * series
    return jnp.where(y > -0.5, -y * series, 1.0 - jnp.exp(y))


def decay_part(off, l_ref, sums_ref, cum_ref, sc_ref, dec_ref):
    extra = jnp.full((PAD - HEADS, Q), -1.0, F32)
    pieces = []
    for c in range(CHUNKS):
        pieces += [l_ref[:, c * Q : (c + 1) * Q], extra]
    l = jnp.concatenate(pieces, axis=0)
    square = jnp.maximum(minus_expm1(2.0 * l), 1.2e-38)
    gain = jnp.sqrt(square)
    lg = jnp.log(square) * 0.5
    high = l.astype(BF16)
    rest = l - high.astype(F32)
    mid = rest.astype(BF16)
    low = (rest - mid.astype(F32)).astype(BF16)
    both = nn(high, sums_ref[...]) + nn(mid, sums_ref[...]) + nn(low, sums_ref[...])
    fwd, rev = both[:, :Q], both[:, Q:]
    cut = lambda a, c: a[c * PAD : (c + 1) * PAD]
    ends = [cut(fwd, c)[:, Q - 1 : Q] for c in range(CHUNKS)]
    before = [jnp.zeros((PAD, 1), F32)]
    for c in range(CHUNKS):
        before.append(before[-1] + ends[c])
    after = [jnp.zeros((PAD, 1), F32)]
    for c in range(CHUNKS - 1, 0, -1):
        after.append(after[-1] + ends[c])
    after = after[::-1]
    last_count = starts_until(off, jnp.int32(TOK - 1))
    lane = lax.broadcasted_iota(jnp.int32, (PAD, Q), 1)
    decs = jnp.zeros((PAD, Q), F32)
    tail = jnp.exp(rev) * gain
    entry = jnp.exp(fwd)
    shift = fwd - lg
    for c in range(CHUNKS):
        seg = starts_until(off, lane + c * Q)
        seg_b = starts_until(off, jnp.int32(c * Q - 1))
        seg_e = starts_until(off, jnp.int32(c * Q + Q - 1))
        tail_c = jnp.where(seg == seg_e, cut(tail, c), 0.0)
        entry_c = jnp.where(seg == seg_b, cut(entry, c), 0.0)
        tail_d = jnp.where(seg == last_count, jnp.exp(cut(rev, c) + after[c]) * cut(gain, c), 0.0)
        entry_d = jnp.where(seg == 0, jnp.exp(cut(fwd, c) + before[c]), 0.0)
        rows = []
        for a in (tail_d, entry_d, tail_c, entry_c):
            hi = a.astype(BF16)
            rows += [hi, (a - hi.astype(F32)).astype(BF16)]
        sc_ref[c * Q : (c + 1) * Q, :] = jnp.concatenate(rows, axis=0).T
        cum_ref[:PAD, c * Q : (c + 1) * Q] = cut(fwd, c)
        cum_ref[PAD:, c * Q : (c + 1) * Q] = cut(shift, c)
        keep_c = jnp.where(seg_b == seg_e, 1.0, 0.0)
        decs = jnp.where(lane == c, jnp.exp(ends[c]) * keep_c, decs)
        keep_after = jnp.where(seg_e == last_count, 1.0, 0.0)
        decs = jnp.where(lane == 32 + c, jnp.exp(after[c]) * keep_after, decs)
    keep = jnp.where(last_count == 0, 1.0, 0.0)
    decs = jnp.where(lane == CHUNKS, jnp.exp(before[CHUNKS]) * keep, decs)
    hi = decs.astype(BF16).astype(F32)
    full = jnp.concatenate([hi, decs - hi, jnp.zeros((Q - 2 * PAD, Q), F32)], axis=0)
    dec_ref[...] = full.T.astype(BF16)


def prepare_kernel(
    off_hbm, l_hbm, sums_hbm, sp_hbm, x_hbm, g_hbm, cum_hbm, sc_hbm, dec_hbm, xt_ref, xt_hbm, ge_hbm,
    off, l_ref, sums_ref, sp_ref, ge_ref, cum_ref, sc_ref, dec_ref, in_sem, first_sem, out_sem, ge_sem,
):
    first = [
        pltpu.make_async_copy(src, dst, first_sem.at[n])
        for n, (src, dst) in enumerate(((l_hbm, l_ref), (off_hbm, off), (sums_hbm, sums_ref), (sp_hbm, sp_ref)))
    ]
    for copy in first:
        copy.start()
    for i in range(BLOCKS):
        block_copy(x_hbm, xt_ref, in_sem, 0, i).start()
        block_copy(g_hbm, ge_ref, in_sem, 1, i).start()
    for copy in first:
        copy.wait()
    decay_part(off, l_ref, sums_ref, cum_ref, sc_ref, dec_ref)
    saves = [
        pltpu.make_async_copy(src, dst, out_sem.at[n])
        for n, (src, dst) in enumerate(((cum_ref, cum_hbm), (sc_ref, sc_hbm), (dec_ref, dec_hbm)))
    ]
    for save in saves:
        save.start()

    @pl.loop(0, BLOCKS)
    def _(i):
        block_copy(x_hbm, xt_ref, in_sem, 0, i).wait()
        block_copy(g_hbm, ge_ref, in_sem, 1, i).wait()
        r = pl.ds(pl.multiple_of(i * BLOCK, BLOCK), BLOCK)
        s = nn(sc_ref[r, :], sp_ref[...])
        ge_ref[r, :] = (ge_ref[r, :].astype(F32) * s[:, WIDTH:]).astype(BF16)
        block_copy(ge_ref, ge_hbm, ge_sem, 0, i).start()
        xt_ref[r, :] = (xt_ref[r, :].astype(F32) * s[:, :WIDTH]).astype(BF16)
        block_copy(xt_ref, xt_hbm, ge_sem, 1, i).start()

    for save in saves:
        save.wait()
    for i in range(BLOCKS):
        block_copy(ge_ref, ge_hbm, ge_sem, 0, i).wait()
        block_copy(xt_ref, xt_hbm, ge_sem, 1, i).wait()


def prepare_call(off, log_decay, sums, sp, x, g):
    return pl.pallas_call(
        prepare_kernel,
        out_shape=(
            far_out((2 * PAD, TOK), F32),
            far_out((TOK, STATE), BF16),
            far_out((STATE, STATE), BF16),
            kept((TOK, WIDTH), BF16),
            far_out((TOK, WIDTH), BF16),
            far_out((TOK, WIDTH), BF16),
        ),
        in_specs=[FAR] * 6,
        out_specs=(FAR, FAR, FAR, WHOLE, FAR, FAR),
        scratch_shapes=[
            pltpu.SMEM((1, 4), jnp.int32),
            pltpu.VMEM((HEADS, TOK), F32),
            pltpu.VMEM((Q, 2 * Q), BF16),
            pltpu.VMEM((STATE, 2 * WIDTH), BF16),
            pltpu.VMEM((TOK, WIDTH), BF16),
            pltpu.VMEM((2 * PAD, TOK), F32),
            pltpu.VMEM((TOK, STATE), BF16),
            pltpu.VMEM((STATE, STATE), BF16),
            pltpu.SemaphoreType.DMA((2, BLOCKS)),
            pltpu.SemaphoreType.DMA((4,)),
            pltpu.SemaphoreType.DMA((3,)),
            pltpu.SemaphoreType.DMA((2, BLOCKS)),
        ],
        compiler_params=options(),
        cost_estimate=cost(4e9, 16e6),
        name="prepare",
    )(*far(off, log_decay, sums, sp, x, g))


def state_kernel(
    place, m0, m1, m2, m3, o0, o1, o2, o3, xt_ref, ge_hbm, dec_hbm, out_ref, bc_hbm,
    ge_ref, bc_ref, dec_ref, s_ref, in_sem, out_sem,
):
    load = pltpu.make_async_copy(ge_hbm, ge_ref, in_sem.at[0])
    load.start()
    dec_load = pltpu.make_async_copy(dec_hbm, dec_ref, in_sem.at[1])
    dec_load.start()
    core, y = place[0], place[1]
    for k, (m, o) in enumerate(((m0, o0), (m1, o1), (m2, o2), (m3, o3))):
        pair = lax.rem(y + 4 - k, 4) * 2
        bc_ref[pl.ds(pl.multiple_of((pair + core) * BLOCK, BLOCK), BLOCK), :] = m[...]
        bc_ref[pl.ds(pl.multiple_of((pair + 1 - core) * BLOCK, BLOCK), BLOCK), :] = o[...]
    saves = [
        pltpu.make_async_copy(src, dst, out_sem.at[n])
        for n, (src, dst) in enumerate(((bc_ref, bc_hbm),))
    ]
    for save in saves:
        save.start()
    rows = TOK // 4
    for first, src, half in ((0, xt_ref, slice(0, STATE)), (16, ge_ref, slice(STATE, 2 * STATE))):
        if first:
            load.wait()
            dec_load.wait()
        for i in range(4):
            part = tn(bc_ref[i * rows : (i + 1) * rows, half], src[i * rows : (i + 1) * rows, :])
            if i == 0:
                s_ref[...] = part
            else:
                s_ref[...] += part
        out_ref[first : first + 16, :, :WIDTH] = s_ref[...].reshape(16, 8, WIDTH).astype(BF16)
    row = dec_ref[CHUNKS : CHUNKS + 1, :].astype(F32)
    out_ref[:, :, WIDTH:] = jnp.broadcast_to(row[None], (32, 8, STATE)).astype(BF16)
    for save in saves:
        save.wait()


def state_call(place, pieces, xt, ge, dec):
    return pl.pallas_call(
        state_kernel,
        out_shape=(
            jax.ShapeDtypeStruct((32, 8, WIDTH + STATE), BF16),
            far_out((TOK, 2 * STATE), BF16),
        ),
        in_specs=[SCALARS] + [WHOLE] * 9 + [FAR, FAR],
        out_specs=(WHOLE, FAR),
        scratch_shapes=[
            pltpu.VMEM((TOK, WIDTH), BF16),
            pltpu.VMEM((TOK, 2 * STATE), BF16),
            pltpu.VMEM((STATE, STATE), BF16),
            pltpu.VMEM((STATE, WIDTH), F32),
            pltpu.SemaphoreType.DMA((2,)),
            pltpu.SemaphoreType.DMA((2,)),
        ],
        compiler_params=options(),
        cost_estimate=cost(7e8, 6.5e6),
        name="states",
    )(place, *pieces, *held(xt), *far(ge, dec))


def scan_kernel(me, in_ref, sp_ref, out_ref, d_ref):
    rows = in_ref[:, :, WIDTH:].astype(F32).reshape(256, STATE).astype(BF16)
    d_ref[...] = nn(rows, sp_ref[...]).reshape(32, 8, WIDTH)
    backward = me[0] >= 16

    def one(k, state):
        b = jnp.where(backward, 31 - k, k)
        out_ref[b] = state.astype(BF16)
        return d_ref[b] * state + in_ref[b, :, :WIDTH].astype(F32)

    lax.fori_loop(0, 32, one, jnp.zeros((8, WIDTH), F32), unroll=True)


def scan_call(me, part, sp):
    vm = pl.BlockSpec(memory_space=pltpu.VMEM)
    return pl.pallas_call(
        scan_kernel,
        out_shape=jax.ShapeDtypeStruct((32, 8, WIDTH), BF16),
        in_specs=[pl.BlockSpec(memory_space=pltpu.SMEM), vm, vm],
        out_specs=vm,
        scratch_shapes=[pltpu.VMEM((32, 8, WIDTH), F32)],
        compiler_params=pltpu.CompilerParams(vmem_limit_bytes=VMEM),
        name="scan",
    )(me, part, sp)


def within_kernel(
    off_hbm, x_hbm, g_hbm, bc_hbm, cum_hbm, skip_ref, gx_hbm, z_hbm,
    off, cum_ref, x_ref, g_ref, bc_ref, gx_ref, z_ref, first_sem, in_sem, out_sem,
):
    first = [
        pltpu.make_async_copy(off_hbm, off, first_sem.at[0]),
        pltpu.make_async_copy(cum_hbm, cum_ref, first_sem.at[1]),
    ]
    for copy in first:
        copy.start()
    def fetch(i):
        block_copy(bc_hbm, bc_ref, in_sem, 2, i).start()
        block_copy(x_hbm, x_ref, in_sem, 0, i).start()
        block_copy(g_hbm, g_ref, in_sem, 1, i).start()

    for i in range(AHEAD):
        fetch(i)
    si = lax.broadcasted_iota(jnp.int32, (Q, Q), 0)
    ti = lax.broadcasted_iota(jnp.int32, (Q, Q), 1)
    even = lax.broadcasted_iota(jnp.int32, (Q, Q), 1) < 64
    odd = jnp.logical_not(even)
    zero = jnp.zeros((Q, Q), BF16)
    for copy in first:
        copy.wait()

    @pl.loop(0, BLOCKS)
    def _(step):
        @pl.when(step + AHEAD < BLOCKS)
        def _():
            fetch(step + AHEAD)

        block_copy(bc_hbm, bc_ref, in_sem, 2, step).wait()
        block_copy(x_hbm, x_ref, in_sem, 0, step).wait()
        block_copy(g_hbm, g_ref, in_sem, 1, step).wait()
        parts = []
        for sub in range(BLOCK // Q):
            base = pl.multiple_of(step * BLOCK + sub * Q, Q)
            r = pl.ds(base, Q)
            same = starts_until(off, si + base) == starts_until(off, ti + base)
            bias = jnp.where((ti >= si) & same, 0.0, NEG)
            parts.append((r, cum_ref[:PAD, r], cum_ref[PAD:, r].T, nt(bc_ref[r, :STATE], bc_ref[r, STATE:]), bias))
        zs = [jnp.zeros((Q, Q), F32)] * len(parts)
        for p in range(HEADS // 2):
            w = slice(p * Q, (p + 1) * Q)
            h = 2 * p
            for n, (r, lt, ls, scores, bias) in enumerate(parts):
                g = g_ref[r, w]
                both = jnp.concatenate([jnp.where(even, g, zero), jnp.where(odd, g, zero)], axis=0)
                e = nt(x_ref[r, w], both)
                ma = jnp.exp(lt[h : h + 1, :] - ls[:, h : h + 1] + bias)
                mb = jnp.exp(lt[h + 1 : h + 2, :] - ls[:, h + 1 : h + 2] + bias)
                zs[n] = zs[n] + (ma * e[:, :Q] + mb * e[:, Q:])
                weights = jnp.concatenate([(ma * scores).astype(BF16), (mb * scores).astype(BF16)], axis=1)
                gx_ref[r, w] = (nn(weights, both) + g.astype(F32) * skip_ref[:, w]).astype(BF16)
        for n, part in enumerate(parts):
            z_ref[part[0], :] = zs[n].astype(BF16)
        block_copy(gx_ref, gx_hbm, out_sem, 0, step).start()
        block_copy(z_ref, z_hbm, out_sem, 1, step).start()

    for i in range(BLOCKS):
        block_copy(gx_ref, gx_hbm, out_sem, 0, i).wait()
        block_copy(z_ref, z_hbm, out_sem, 1, i).wait()


def within_call(off, x, g, bc, cum, skip):
    return pl.pallas_call(
        within_kernel,
        out_shape=(far_out((TOK, WIDTH), BF16), far_out((TOK, STATE), BF16)),
        in_specs=[FAR] * 5 + [WHOLE],
        out_specs=(FAR, FAR),
        scratch_shapes=[
            pltpu.SMEM((1, 4), jnp.int32),
            pltpu.VMEM((2 * PAD, TOK), F32),
            pltpu.VMEM((TOK, WIDTH), BF16),
            pltpu.VMEM((TOK, WIDTH), BF16),
            pltpu.VMEM((TOK, 2 * STATE), BF16),
            pltpu.VMEM((TOK, WIDTH), BF16),
            pltpu.VMEM((TOK, STATE), BF16),
            pltpu.SemaphoreType.DMA((2,)),
            pltpu.SemaphoreType.DMA((3, BLOCKS)),
            pltpu.SemaphoreType.DMA((2, BLOCKS)),
        ],
        compiler_params=options(),
        cost_estimate=cost(4e9, 16e6),
        name="within_chunks",
    )(*far(off, x, g, bc, cum), skip)


def chain_kernel(
    x_hbm, g_hbm, bc_hbm, sc_hbm, z_hbm, xt_hbm, dec_ref, sp_ref, spf_ref, gc_hbm, gb_hbm, tst_hbm, xt_ref,
    x_ref, g_ref, bc_ref, sc_ref, z_ref, gc_ref, gb_ref, tst_ref, s_ref, t_ref, d_ref, in_sem, out_sem, next_sem,
):
    loads = ((sc_hbm, sc_ref), (x_hbm, x_ref), (g_hbm, g_ref), (bc_hbm, bc_ref), (z_hbm, z_ref))
    for i in range(BLOCKS // 2):
        for j in (i, BLOCKS - 1 - i):
            for n, (src, dst) in enumerate(loads):
                block_copy(src, dst, in_sem, n, j).start()
    ahead = pltpu.make_async_copy(xt_hbm, xt_ref, next_sem)
    ahead.start()
    s_ref[...] = jnp.zeros_like(s_ref)
    t_ref[...] = jnp.zeros_like(t_ref)
    d_ref[...] = nn(dec_ref[:CHUNKS, :], spf_ref[...])
    per = BLOCK // Q

    def advance(step, fresh):
        if fresh:
            for j in (step, BLOCKS - 1 - step):
                for n, (src, dst) in enumerate(loads):
                    block_copy(src, dst, in_sem, n, j).wait()
                for sub in range(per):
                    r = pl.ds(pl.multiple_of(j * BLOCK + sub * Q, Q), Q)
                    s = nn(sc_ref[r, :], sp_ref[...])
                    x_ref[r, :] = (x_ref[r, :].astype(F32) * s[:, :WIDTH]).astype(BF16)
                    g_ref[r, :] = (g_ref[r, :].astype(F32) * s[:, WIDTH:]).astype(BF16)

        back = BLOCKS - 1 - step
        for sub in range(per):
            c = step * per + sub
            r = pl.ds(pl.multiple_of(c * Q, Q), Q)
            state = s_ref[...]
            b = bc_ref[r, :STATE]
            gc_ref[r, :] = tn(z_ref[r, :], b) + nt(g_ref[r, :], state.astype(BF16))
            s_ref[...] = d_ref[pl.ds(c, 1), :] * state + tn(b, x_ref[r, :])
            c = back * per + per - 1 - sub
            r = pl.ds(pl.multiple_of(c * Q, Q), Q)
            state = t_ref[...]
            low = state.astype(BF16)
            tst_ref[c] = low
            q = bc_ref[r, STATE:]
            gb_ref[r, :] = nn(z_ref[r, :], q) + nt(x_ref[r, :], low)
            t_ref[...] = d_ref[pl.ds(c, 1), :] * state + tn(q, g_ref[r, :])
        block_copy(gc_ref, gc_hbm, out_sem, 0, step).start()
        block_copy(gb_ref, gb_hbm, out_sem, 1, back).start()
        block_copy(tst_ref, tst_hbm, out_sem, 2, back, per).start()

    @pl.loop(0, BLOCKS // 2)
    def _(step):
        advance(step, True)

    @pl.loop(BLOCKS // 2, BLOCKS)
    def _(step):
        advance(step, False)

    for i in range(BLOCKS):
        block_copy(gc_ref, gc_hbm, out_sem, 0, i).wait()
        block_copy(gb_ref, gb_hbm, out_sem, 1, i).wait()
        block_copy(tst_ref, tst_hbm, out_sem, 2, i, per).wait()
    ahead.wait()


def chain_call(x, g, bc, sc, z, xt, dec, sp, spf):
    return pl.pallas_call(
        chain_kernel,
        out_shape=(
            far_out((TOK, STATE), F32),
            far_out((TOK, STATE), F32),
            far_out((CHUNKS, STATE, WIDTH), BF16),
            kept((TOK, WIDTH), BF16),
        ),
        in_specs=[FAR] * 6 + [WHOLE] * 3,
        out_specs=(FAR, FAR, FAR, WHOLE),
        scratch_shapes=[
            pltpu.VMEM((TOK, WIDTH), BF16),
            pltpu.VMEM((TOK, WIDTH), BF16),
            pltpu.VMEM((TOK, 2 * STATE), BF16),
            pltpu.VMEM((TOK, STATE), BF16),
            pltpu.VMEM((TOK, STATE), BF16),
            pltpu.VMEM((TOK, STATE), F32),
            pltpu.VMEM((TOK, STATE), F32),
            pltpu.VMEM((CHUNKS, STATE, WIDTH), BF16),
            pltpu.VMEM((STATE, WIDTH), F32),
            pltpu.VMEM((STATE, WIDTH), F32),
            pltpu.VMEM((CHUNKS, WIDTH), F32),
            pltpu.SemaphoreType.DMA((5, BLOCKS)),
            pltpu.SemaphoreType.DMA((3, BLOCKS)),
            pltpu.SemaphoreType.DMA,
        ],
        compiler_params=options(),
        cost_estimate=cost(4e9, 16e6),
        name="chunk_chain",
    )(*far(x, g, bc, sc, z, xt), dec, sp, spf)


def carry_kernel(place, xt_ref, ge_hbm, gb_hbm, gc_hbm, st_ref, keep_ref, send_ref, ge_ref, gb_ref, gc_ref, in_sem):
    core = place[0]
    loads = ((gb_hbm, gb_ref), (gc_hbm, gc_ref), (ge_hbm, ge_ref))
    for n, (src, dst) in enumerate(loads):
        for i in range(4):
            block_copy(src, dst, in_sem, n, i, 2 * BLOCK).start()
    s = st_ref[:STATE, :]
    t = st_ref[STATE:, :]
    for i in range(4):
        block_copy(gb_hbm, gb_ref, in_sem, 0, i, 2 * BLOCK).wait()
        r = pl.ds(pl.multiple_of((2 * i + core) * BLOCK, BLOCK), BLOCK)
        keep_ref[i, :, :STATE] = gb_ref[r, :] + nt(xt_ref[r, :], t)
        r = pl.ds(pl.multiple_of((2 * i + 1 - core) * BLOCK, BLOCK), BLOCK)
        send_ref[i, :, :STATE] = (gb_ref[r, :] + nt(xt_ref[r, :], t)).astype(BF16)
    for i in range(4):
        block_copy(gc_hbm, gc_ref, in_sem, 1, i, 2 * BLOCK).wait()
        block_copy(ge_hbm, ge_ref, in_sem, 2, i, 2 * BLOCK).wait()
        r = pl.ds(pl.multiple_of((2 * i + core) * BLOCK, BLOCK), BLOCK)
        keep_ref[i, :, STATE:] = gc_ref[r, :] + nt(ge_ref[r, :], s)
        r = pl.ds(pl.multiple_of((2 * i + 1 - core) * BLOCK, BLOCK), BLOCK)
        send_ref[i, :, STATE:] = (gc_ref[r, :] + nt(ge_ref[r, :], s)).astype(BF16)


def carry_call(place, xt, ge, gb, gc, st):
    return pl.pallas_call(
        carry_kernel,
        out_shape=(
            jax.ShapeDtypeStruct((4, BLOCK, 2 * STATE), F32),
            jax.ShapeDtypeStruct((4, BLOCK, 2 * STATE), BF16),
        ),
        in_specs=[SCALARS, WHOLE, FAR, FAR, FAR, WHOLE],
        out_specs=(WHOLE, WHOLE),
        scratch_shapes=[
            pltpu.VMEM((TOK, WIDTH), BF16),
            pltpu.VMEM((TOK, STATE), F32),
            pltpu.VMEM((TOK, STATE), F32),
            pltpu.SemaphoreType.DMA((3, 4)),
        ],
        compiler_params=options(),
        cost_estimate=cost(7e8, 9e6),
        name="carry",
    )(place, *held(xt), *far(ge, gb, gc), st)


def input_kernel(
    gx_hbm, tst_hbm, bc_hbm, sc_hbm, st_ref, sp_ref, dec_ref, spf_ref, out_hbm,
    gx_ref, tst_ref, bc_ref, sc_ref, d_ref, in_sem, out_sem,
):
    per = BLOCK // Q
    loads = ((gx_hbm, gx_ref, BLOCK), (tst_hbm, tst_ref, per), (bc_hbm, bc_ref, BLOCK), (sc_hbm, sc_ref, BLOCK))
    for i in range(BLOCKS):
        for n, (src, dst, rows) in enumerate(loads):
            block_copy(src, dst, in_sem, n, i, rows).start()
    d_ref[...] = nn(dec_ref[32 : 32 + CHUNKS, :], spf_ref[...])

    @pl.loop(0, BLOCKS)
    def _(step):
        for n, (src, dst, rows) in enumerate(loads):
            block_copy(src, dst, in_sem, n, step, rows).wait()
        for sub in range(per):
            c = step * per + sub
            r = pl.ds(pl.multiple_of(c * Q, Q), Q)
            full = tst_ref[c].astype(F32) + d_ref[pl.ds(c, 1), :] * st_ref[STATE:, :].astype(F32)
            scale = nn(sc_ref[r, :], sp_ref[:, :WIDTH])
            gx_ref[r, :] = (gx_ref[r, :].astype(F32) + scale * nn(bc_ref[r, :STATE], full.astype(BF16))).astype(BF16)
        block_copy(gx_ref, out_hbm, out_sem, 0, step).start()

    for i in range(BLOCKS):
        block_copy(gx_ref, out_hbm, out_sem, 0, i).wait()


def input_call(gx, tst, st, bc, sc, sp, dec, spf):
    return pl.pallas_call(
        input_kernel,
        out_shape=jax.ShapeDtypeStruct((TOK, WIDTH), BF16),
        in_specs=[FAR] * 4 + [WHOLE] * 4,
        out_specs=FAR,
        scratch_shapes=[
            pltpu.VMEM((TOK, WIDTH), BF16),
            pltpu.VMEM((CHUNKS, STATE, WIDTH), BF16),
            pltpu.VMEM((TOK, 2 * STATE), BF16),
            pltpu.VMEM((TOK, STATE), BF16),
            pltpu.VMEM((CHUNKS, WIDTH), F32),
            pltpu.SemaphoreType.DMA((4, BLOCKS)),
            pltpu.SemaphoreType.DMA((1, BLOCKS)),
        ],
        compiler_params=options(),
        cost_estimate=cost(2e9, 12e6),
        name="input_gradient",
    )(*far(gx, tst, bc, sc), st, sp, dec, spf)


def join_kernel(a_hbm, b_hbm, out_ref, sem):
    loads = [
        pltpu.make_async_copy(a_hbm, out_ref.at[:, :STATE], sem.at[0]),
        pltpu.make_async_copy(b_hbm, out_ref.at[:, STATE:], sem.at[1]),
    ]
    for load in loads:
        load.start()
    for load in loads:
        load.wait()


def join_call(a, b):
    return pl.pallas_call(
        join_kernel,
        out_shape=jax.ShapeDtypeStruct((BLOCK, 2 * STATE), BF16),
        in_specs=[FAR, FAR],
        out_specs=WHOLE,
        scratch_shapes=[pltpu.SemaphoreType.DMA((2,))],
        compiler_params=options(),
        name="join",
    )(*far(a, b))


def pair_kernel(place, keep_ref, got_ref, o0, o1, o2, o3):
    y = place[1]
    for k, o in enumerate((o0, o1, o2, o3)):
        j = lax.rem(y + k, 4)
        o[...] = (keep_ref[j] + got_ref[j].astype(F32)).astype(o.dtype)


def pair_call(place, keep, got):
    return pl.pallas_call(
        pair_kernel,
        out_shape=(jax.ShapeDtypeStruct((BLOCK, 2 * STATE), F32),)
        + (jax.ShapeDtypeStruct((BLOCK, 2 * STATE), BF16),) * 3,
        in_specs=[SCALARS, WHOLE, WHOLE],
        out_specs=(WHOLE,) * 4,
        compiler_params=options(),
        name="pair_sums",
    )(place, keep, got)


def total_kernel(a_ref, b_ref, c_ref, d_ref, w_ref, r_ref):
    t = a_ref[...] + b_ref[...].astype(F32) + c_ref[...].astype(F32) + d_ref[...].astype(F32)
    w_ref[...] = t[:, :STATE]
    r_ref[...] = t[:, STATE:]


def total_call(*parts):
    return pl.pallas_call(
        total_kernel,
        out_shape=(jax.ShapeDtypeStruct((BLOCK, STATE), F32),) * 2,
        compiler_params=options(),
        name="totals",
    )(*parts)


def along_y(k):
    return [(i, (i + 2 * k) % 8) for i in range(8)]


SWAP = [(i, i ^ 1) for i in range(8)]


def shards(mixer_input, write_rows, read_rows, log_decay, skip_gain, reset_offsets, grad_out):
    spot = lax.axis_index("head").astype(jnp.int32)
    core, y = spot & 1, spot >> 1
    place = jnp.stack([core, y])
    me = lax.axis_index("seq").astype(jnp.int32).reshape(1)
    spread_d, spread_c, spread_f = (jnp.asarray(a, BF16) for a in (SPREAD_D, SPREAD_C, SPREAD_F))
    own = join_call(write_rows, read_rows)
    mine = [own] + [lax.ppermute(own, "head", along_y(k)) for k in (1, 2, 3)]
    cum, sc, dec, xt, xt_far, ge = prepare_call(
        reset_offsets, log_decay, jnp.asarray(SUMS, BF16), spread_d, mixer_input, grad_out
    )
    *mine, xt, ge = lax.optimization_barrier((*mine, xt, ge))
    other = [lax.ppermute(a, "head", SWAP) for a in mine]
    payload, bc = state_call(place, mine + other, xt, ge, dec)
    parts = lax.all_to_all(payload, "seq", 0, 0, tiled=True)
    skip = jnp.repeat(skip_gain, 64)[None, :]
    gx, z = within_call(reset_offsets, mixer_input, grad_out, bc, cum, skip)
    parts, gx, z = lax.optimization_barrier((parts, gx, z))
    entering = scan_call(me, parts, spread_f)
    st = lax.all_to_all(entering, "seq", 0, 0, tiled=True).reshape(2 * STATE, WIDTH)
    gc, gb, tst, xt = chain_call(
        mixer_input, grad_out, bc, sc, z, xt_far, dec, spread_c, spread_f
    )
    keep, send = carry_call(place, xt, ge, gb, gc, st)
    total, *leaving = pair_call(place, keep, lax.ppermute(send, "head", SWAP))
    arrived = [lax.ppermute(a, "head", along_y(k)) for k, a in zip((1, 2, 3), leaving)]
    grad_input = input_call(gx, tst, st, bc, sc, spread_c, dec, spread_f)
    return (grad_input, *total_call(total, *arrived))


def solution(mesh):
    in_specs = (
        P("seq", "head"),
        P(("seq", "head"), None),
        P(("seq", "head"), None),
        P("head", "seq"),
        P("head"),
        P("seq", None),
        P("seq", "head"),
    )
    out_specs = (P("seq", "head"), P(("seq", "head"), None), P(("seq", "head"), None))
    return jax.shard_map(shards, mesh=mesh, in_specs=in_specs, out_specs=out_specs, check_vma=False)
```

```python
import functools

import jax
import jax.numpy as jnp
import numpy as np
from jax import lax
from jax.experimental import pallas as pl
from jax.experimental.pallas import tpu as pltpu
from jax.sharding import PartitionSpec as P

F32 = jnp.float32
BF16 = jnp.bfloat16
TOK = 2048
HEADS = 10
PAD = 16
WIDTH = 640
STATE = 128
Q = 128
CHUNKS = TOK // Q
BLOCK = 256
BLOCKS = TOK // BLOCK
VMEM = 28 * 1024 * 1024
NEG = -1e30
AHEAD = 2


def spread(first):
    out = np.zeros((STATE, WIDTH), np.float32)
    for j in range(WIDTH):
        out[first + j // 64, j] = 1.0
        out[first + PAD + j // 64, j] = 1.0
    return out


SPREAD_D = np.concatenate([spread(0), spread(32)], axis=1)
SPREAD_C = np.concatenate([spread(64), spread(96)], axis=1)
SPREAD_F = spread(0)
SUMS = np.concatenate([np.triu(np.ones((Q, Q))), np.tril(np.ones((Q, Q)), -1)], axis=1).astype(np.float32)


def nt(a, b):
    return lax.dot_general(a, b, (((1,), (1,)), ((), ())), preferred_element_type=F32)


def tn(a, b):
    return lax.dot_general(a, b, (((0,), (0,)), ((), ())), preferred_element_type=F32)


def nn(a, b):
    return lax.dot_general(a, b, (((1,), (0,)), ((), ())), preferred_element_type=F32)


WHOLE = pl.BlockSpec(memory_space=pltpu.VMEM)
SCALARS = pl.BlockSpec(memory_space=pltpu.SMEM)
FAR = pl.BlockSpec(memory_space=pltpu.HBM)


def far(*arrays):
    return [pltpu.with_memory_space_constraint(a, pltpu.HBM) for a in arrays]


def kept(shape, dtype):
    return pltpu.VMEM(shape, dtype)


def held(*arrays):
    return [pltpu.with_memory_space_constraint(a, pltpu.VMEM) for a in arrays]


def far_out(shape, dtype):
    return pltpu.HBM(shape, dtype)


def block_copy(src, dst, sem, which, i, rows=BLOCK):
    r = pl.ds(pl.multiple_of(i * rows, rows), rows)
    return pltpu.make_async_copy(src.at[r], dst.at[r], sem.at[which, i])


def options():
    return pltpu.CompilerParams(vmem_limit_bytes=VMEM)


def cost(flops, moved):
    return pl.CostEstimate(flops=int(flops), bytes_accessed=int(moved), transcendentals=0)


def starts_until(off, t):
    count = jnp.where(t >= off[0, 0], 1, 0)
    for i in range(1, 4):
        count = count + jnp.where(t >= off[0, i], 1, 0)
    return count


def minus_expm1(y):
    series = 1.0 + y * (1.0 / 10)
    for n in range(9, 1, -1):
        series = 1.0 + y * (1.0 / n) * series
    return jnp.where(y > -0.5, -y * series, 1.0 - jnp.exp(y))


def decay_part(off, l_ref, sums_ref, cum_ref, sc_ref, dec_ref):
    extra = jnp.full((PAD - HEADS, Q), -1.0, F32)
    pieces = []
    for c in range(CHUNKS):
        pieces += [l_ref[:, c * Q : (c + 1) * Q], extra]
    l = jnp.concatenate(pieces, axis=0)
    square = jnp.maximum(minus_expm1(2.0 * l), 1.2e-38)
    gain = jnp.sqrt(square)
    lg = jnp.log(square) * 0.5
    high = l.astype(BF16)
    rest = l - high.astype(F32)
    mid = rest.astype(BF16)
    low = (rest - mid.astype(F32)).astype(BF16)
    both = nn(high, sums_ref[...]) + nn(mid, sums_ref[...]) + nn(low, sums_ref[...])
    fwd, rev = both[:, :Q], both[:, Q:]
    cut = lambda a, c: a[c * PAD : (c + 1) * PAD]
    ends = [cut(fwd, c)[:, Q - 1 : Q] for c in range(CHUNKS)]
    before = [jnp.zeros((PAD, 1), F32)]
    for c in range(CHUNKS):
        before.append(before[-1] + ends[c])
    after = [jnp.zeros((PAD, 1), F32)]
    for c in range(CHUNKS - 1, 0, -1):
        after.append(after[-1] + ends[c])
    after = after[::-1]
    last_count = starts_until(off, jnp.int32(TOK - 1))
    lane = lax.broadcasted_iota(jnp.int32, (PAD, Q), 1)
    decs = jnp.zeros((PAD, Q), F32)
    tail = jnp.exp(rev) * gain
    entry = jnp.exp(fwd)
    shift = fwd - lg
    for c in range(CHUNKS):
        seg = starts_until(off, lane + c * Q)
        seg_b = starts_until(off, jnp.int32(c * Q - 1))
        seg_e = starts_until(off, jnp.int32(c * Q + Q - 1))
        tail_c = jnp.where(seg == seg_e, cut(tail, c), 0.0)
        entry_c = jnp.where(seg == seg_b, cut(entry, c), 0.0)
        tail_d = jnp.where(seg == last_count, jnp.exp(cut(rev, c) + after[c]) * cut(gain, c), 0.0)
        entry_d = jnp.where(seg == 0, jnp.exp(cut(fwd, c) + before[c]), 0.0)
        rows = []
        for a in (tail_d, entry_d, tail_c, entry_c):
            hi = a.astype(BF16)
            rows += [hi, (a - hi.astype(F32)).astype(BF16)]
        sc_ref[c * Q : (c + 1) * Q, :] = jnp.concatenate(rows, axis=0).T
        cum_ref[:PAD, c * Q : (c + 1) * Q] = cut(fwd, c)
        cum_ref[PAD:, c * Q : (c + 1) * Q] = cut(shift, c)
        keep_c = jnp.where(seg_b == seg_e, 1.0, 0.0)
        decs = jnp.where(lane == c, jnp.exp(ends[c]) * keep_c, decs)
        keep_after = jnp.where(seg_e == last_count, 1.0, 0.0)
        decs = jnp.where(lane == 32 + c, jnp.exp(after[c]) * keep_after, decs)
    keep = jnp.where(last_count == 0, 1.0, 0.0)
    decs = jnp.where(lane == CHUNKS, jnp.exp(before[CHUNKS]) * keep, decs)
    hi = decs.astype(BF16).astype(F32)
    full = jnp.concatenate([hi, decs - hi, jnp.zeros((Q - 2 * PAD, Q), F32)], axis=0)
    dec_ref[...] = full.T.astype(BF16)


def prepare_kernel(
    off_hbm, l_hbm, sums_hbm, sp_hbm, x_hbm, g_hbm, cum_hbm, sc_hbm, dec_hbm, xt_ref, xt_hbm, ge_hbm,
    off, l_ref, sums_ref, sp_ref, ge_ref, cum_ref, sc_ref, dec_ref, in_sem, first_sem, out_sem, ge_sem,
):
    first = [
        pltpu.make_async_copy(src, dst, first_sem.at[n])
        for n, (src, dst) in enumerate(((l_hbm, l_ref), (off_hbm, off), (sums_hbm, sums_ref), (sp_hbm, sp_ref)))
    ]
    for copy in first:
        copy.start()
    for i in range(BLOCKS):
        block_copy(x_hbm, xt_ref, in_sem, 0, i).start()
        block_copy(g_hbm, ge_ref, in_sem, 1, i).start()
    for copy in first:
        copy.wait()
    decay_part(off, l_ref, sums_ref, cum_ref, sc_ref, dec_ref)
    saves = [
        pltpu.make_async_copy(src, dst, out_sem.at[n])
        for n, (src, dst) in enumerate(((cum_ref, cum_hbm), (sc_ref, sc_hbm), (dec_ref, dec_hbm)))
    ]
    for save in saves:
        save.start()

    @pl.loop(0, BLOCKS)
    def _(i):
        block_copy(x_hbm, xt_ref, in_sem, 0, i).wait()
        block_copy(g_hbm, ge_ref, in_sem, 1, i).wait()
        r = pl.ds(pl.multiple_of(i * BLOCK, BLOCK), BLOCK)
        s = nn(sc_ref[r, :], sp_ref[...])
        ge_ref[r, :] = (ge_ref[r, :].astype(F32) * s[:, WIDTH:]).astype(BF16)
        block_copy(ge_ref, ge_hbm, ge_sem, 0, i).start()
        xt_ref[r, :] = (xt_ref[r, :].astype(F32) * s[:, :WIDTH]).astype(BF16)
        block_copy(xt_ref, xt_hbm, ge_sem, 1, i).start()

    for save in saves:
        save.wait()
    for i in range(BLOCKS):
        block_copy(ge_ref, ge_hbm, ge_sem, 0, i).wait()
        block_copy(xt_ref, xt_hbm, ge_sem, 1, i).wait()


def prepare_call(off, log_decay, sums, sp, x, g):
    return pl.pallas_call(
        prepare_kernel,
        out_shape=(
            far_out((2 * PAD, TOK), F32),
            far_out((TOK, STATE), BF16),
            far_out((STATE, STATE), BF16),
            kept((TOK, WIDTH), BF16),
            far_out((TOK, WIDTH), BF16),
            far_out((TOK, WIDTH), BF16),
        ),
        in_specs=[FAR] * 6,
        out_specs=(FAR, FAR, FAR, WHOLE, FAR, FAR),
        scratch_shapes=[
            pltpu.SMEM((1, 4), jnp.int32),
            pltpu.VMEM((HEADS, TOK), F32),
            pltpu.VMEM((Q, 2 * Q), BF16),
            pltpu.VMEM((STATE, 2 * WIDTH), BF16),
            pltpu.VMEM((TOK, WIDTH), BF16),
            pltpu.VMEM((2 * PAD, TOK), F32),
            pltpu.VMEM((TOK, STATE), BF16),
            pltpu.VMEM((STATE, STATE), BF16),
            pltpu.SemaphoreType.DMA((2, BLOCKS)),
            pltpu.SemaphoreType.DMA((4,)),
            pltpu.SemaphoreType.DMA((3,)),
            pltpu.SemaphoreType.DMA((2, BLOCKS)),
        ],
        compiler_params=options(),
        cost_estimate=cost(4e9, 16e6),
        name="prepare",
    )(*far(off, log_decay, sums, sp, x, g))


def state_kernel(
    place, m0, m1, m2, m3, o0, o1, o2, o3, xt_ref, ge_hbm, dec_hbm, out_ref, bc_hbm,
    ge_ref, bc_ref, dec_ref, s_ref, in_sem, out_sem,
):
    load = pltpu.make_async_copy(ge_hbm, ge_ref, in_sem.at[0])
    load.start()
    dec_load = pltpu.make_async_copy(dec_hbm, dec_ref, in_sem.at[1])
    dec_load.start()
    core, y = place[0], place[1]
    for k, (m, o) in enumerate(((m0, o0), (m1, o1), (m2, o2), (m3, o3))):
        pair = lax.rem(y + 4 - k, 4) * 2
        bc_ref[pl.ds(pl.multiple_of((pair + core) * BLOCK, BLOCK), BLOCK), :] = m[...]
        bc_ref[pl.ds(pl.multiple_of((pair + 1 - core) * BLOCK, BLOCK), BLOCK), :] = o[...]
    saves = [
        pltpu.make_async_copy(src, dst, out_sem.at[n])
        for n, (src, dst) in enumerate(((bc_ref, bc_hbm),))
    ]
    for save in saves:
        save.start()
    rows = TOK // 4
    for first, src, half in ((0, xt_ref, slice(0, STATE)), (16, ge_ref, slice(STATE, 2 * STATE))):
        if first:
            load.wait()
            dec_load.wait()
        for i in range(4):
            part = tn(bc_ref[i * rows : (i + 1) * rows, half], src[i * rows : (i + 1) * rows, :])
            if i == 0:
                s_ref[...] = part
            else:
                s_ref[...] += part
        out_ref[first : first + 16, :, :WIDTH] = s_ref[...].reshape(16, 8, WIDTH).astype(BF16)
    row = dec_ref[CHUNKS : CHUNKS + 1, :].astype(F32)
    out_ref[:, :, WIDTH:] = jnp.broadcast_to(row[None], (32, 8, STATE)).astype(BF16)
    for save in saves:
        save.wait()


def state_call(place, pieces, xt, ge, dec):
    return pl.pallas_call(
        state_kernel,
        out_shape=(
            jax.ShapeDtypeStruct((32, 8, WIDTH + STATE), BF16),
            far_out((TOK, 2 * STATE), BF16),
        ),
        in_specs=[SCALARS] + [WHOLE] * 9 + [FAR, FAR],
        out_specs=(WHOLE, FAR),
        scratch_shapes=[
            pltpu.VMEM((TOK, WIDTH), BF16),
            pltpu.VMEM((TOK, 2 * STATE), BF16),
            pltpu.VMEM((STATE, STATE), BF16),
            pltpu.VMEM((STATE, WIDTH), F32),
            pltpu.SemaphoreType.DMA((2,)),
            pltpu.SemaphoreType.DMA((2,)),
        ],
        compiler_params=options(),
        cost_estimate=cost(7e8, 6.5e6),
        name="states",
    )(place, *pieces, *held(xt), *far(ge, dec))


def scan_kernel(me, in_ref, sp_ref, out_ref, d_ref):
    rows = in_ref[:, :, WIDTH:].astype(F32).reshape(256, STATE).astype(BF16)
    d_ref[...] = nn(rows, sp_ref[...]).reshape(32, 8, WIDTH)
    backward = me[0] >= 16

    def one(k, state):
        b = jnp.where(backward, 31 - k, k)
        out_ref[b] = state.astype(BF16)
        return d_ref[b] * state + in_ref[b, :, :WIDTH].astype(F32)

    lax.fori_loop(0, 32, one, jnp.zeros((8, WIDTH), F32), unroll=True)


def scan_call(me, part, sp):
    vm = pl.BlockSpec(memory_space=pltpu.VMEM)
    return pl.pallas_call(
        scan_kernel,
        out_shape=jax.ShapeDtypeStruct((32, 8, WIDTH), BF16),
        in_specs=[pl.BlockSpec(memory_space=pltpu.SMEM), vm, vm],
        out_specs=vm,
        scratch_shapes=[pltpu.VMEM((32, 8, WIDTH), F32)],
        compiler_params=pltpu.CompilerParams(vmem_limit_bytes=VMEM),
        name="scan",
    )(me, part, sp)


def within_kernel(
    off_hbm, x_hbm, g_hbm, bc_hbm, cum_hbm, skip_ref, gx_hbm, z_hbm,
    off, cum_ref, x_ref, g_ref, bc_ref, gx_ref, z_ref, first_sem, in_sem, out_sem,
):
    first = [
        pltpu.make_async_copy(off_hbm, off, first_sem.at[0]),
        pltpu.make_async_copy(cum_hbm, cum_ref, first_sem.at[1]),
    ]
    for copy in first:
        copy.start()
    def fetch(i):
        block_copy(bc_hbm, bc_ref, in_sem, 2, i).start()
        block_copy(x_hbm, x_ref, in_sem, 0, i).start()
        block_copy(g_hbm, g_ref, in_sem, 1, i).start()

    for i in range(AHEAD):
        fetch(i)
    si = lax.broadcasted_iota(jnp.int32, (Q, Q), 0)
    ti = lax.broadcasted_iota(jnp.int32, (Q, Q), 1)
    even = lax.broadcasted_iota(jnp.int32, (Q, Q), 1) < 64
    odd = jnp.logical_not(even)
    zero = jnp.zeros((Q, Q), BF16)
    for copy in first:
        copy.wait()

    @pl.loop(0, BLOCKS)
    def _(step):
        @pl.when(step + AHEAD < BLOCKS)
        def _():
            fetch(step + AHEAD)

        block_copy(bc_hbm, bc_ref, in_sem, 2, step).wait()
        block_copy(x_hbm, x_ref, in_sem, 0, step).wait()
        block_copy(g_hbm, g_ref, in_sem, 1, step).wait()
        parts = []
        for sub in range(BLOCK // Q):
            base = pl.multiple_of(step * BLOCK + sub * Q, Q)
            r = pl.ds(base, Q)
            same = starts_until(off, si + base) == starts_until(off, ti + base)
            bias = jnp.where((ti >= si) & same, 0.0, NEG)
            parts.append((r, cum_ref[:PAD, r], cum_ref[PAD:, r].T, nt(bc_ref[r, :STATE], bc_ref[r, STATE:]), bias))
        zs = [jnp.zeros((Q, Q), F32)] * len(parts)
        for p in range(HEADS // 2):
            w = slice(p * Q, (p + 1) * Q)
            h = 2 * p
            for n, (r, lt, ls, scores, bias) in enumerate(parts):
                g = g_ref[r, w]
                both = jnp.concatenate([jnp.where(even, g, zero), jnp.where(odd, g, zero)], axis=0)
                e = nt(x_ref[r, w], both)
                ma = jnp.exp(lt[h : h + 1, :] - ls[:, h : h + 1] + bias)
                mb = jnp.exp(lt[h + 1 : h + 2, :] - ls[:, h + 1 : h + 2] + bias)
                zs[n] = zs[n] + (ma * e[:, :Q] + mb * e[:, Q:])
                weights = jnp.concatenate([(ma * scores).astype(BF16), (mb * scores).astype(BF16)], axis=1)
                gx_ref[r, w] = (nn(weights, both) + g.astype(F32) * skip_ref[:, w]).astype(BF16)
        for n, part in enumerate(parts):
            z_ref[part[0], :] = zs[n].astype(BF16)
        block_copy(gx_ref, gx_hbm, out_sem, 0, step).start()
        block_copy(z_ref, z_hbm, out_sem, 1, step).start()

    for i in range(BLOCKS):
        block_copy(gx_ref, gx_hbm, out_sem, 0, i).wait()
        block_copy(z_ref, z_hbm, out_sem, 1, i).wait()


def within_call(off, x, g, bc, cum, skip):
    return pl.pallas_call(
        within_kernel,
        out_shape=(far_out((TOK, WIDTH), BF16), far_out((TOK, STATE), BF16)),
        in_specs=[FAR] * 5 + [WHOLE],
        out_specs=(FAR, FAR),
        scratch_shapes=[
            pltpu.SMEM((1, 4), jnp.int32),
            pltpu.VMEM((2 * PAD, TOK), F32),
            pltpu.VMEM((TOK, WIDTH), BF16),
            pltpu.VMEM((TOK, WIDTH), BF16),
            pltpu.VMEM((TOK, 2 * STATE), BF16),
            pltpu.VMEM((TOK, WIDTH), BF16),
            pltpu.VMEM((TOK, STATE), BF16),
            pltpu.SemaphoreType.DMA((2,)),
            pltpu.SemaphoreType.DMA((3, BLOCKS)),
            pltpu.SemaphoreType.DMA((2, BLOCKS)),
        ],
        compiler_params=options(),
        cost_estimate=cost(4e9, 16e6),
        name="within_chunks",
    )(*far(off, x, g, bc, cum), skip)


def chain_kernel(
    x_hbm, g_hbm, bc_hbm, sc_hbm, z_hbm, xt_hbm, dec_ref, sp_ref, spf_ref, gc_hbm, gb_hbm, tst_hbm, xt_ref,
    x_ref, g_ref, bc_ref, sc_ref, z_ref, gc_ref, gb_ref, tst_ref, s_ref, t_ref, d_ref, in_sem, out_sem, next_sem,
):
    loads = ((sc_hbm, sc_ref), (x_hbm, x_ref), (g_hbm, g_ref), (bc_hbm, bc_ref), (z_hbm, z_ref))
    for i in range(BLOCKS // 2):
        for j in (i, BLOCKS - 1 - i):
            for n, (src, dst) in enumerate(loads):
                block_copy(src, dst, in_sem, n, j).start()
    ahead = pltpu.make_async_copy(xt_hbm, xt_ref, next_sem)
    ahead.start()
    s_ref[...] = jnp.zeros_like(s_ref)
    t_ref[...] = jnp.zeros_like(t_ref)
    d_ref[...] = nn(dec_ref[:CHUNKS, :], spf_ref[...])
    per = BLOCK // Q

    def advance(step, fresh):
        if fresh:
            for j in (step, BLOCKS - 1 - step):
                for n, (src, dst) in enumerate(loads):
                    block_copy(src, dst, in_sem, n, j).wait()
                for sub in range(per):
                    r = pl.ds(pl.multiple_of(j * BLOCK + sub * Q, Q), Q)
                    s = nn(sc_ref[r, :], sp_ref[...])
                    x_ref[r, :] = (x_ref[r, :].astype(F32) * s[:, :WIDTH]).astype(BF16)
                    g_ref[r, :] = (g_ref[r, :].astype(F32) * s[:, WIDTH:]).astype(BF16)

        back = BLOCKS - 1 - step
        for sub in range(per):
            c = step * per + sub
            r = pl.ds(pl.multiple_of(c * Q, Q), Q)
            state = s_ref[...]
            b = bc_ref[r, :STATE]
            gc_ref[r, :] = (tn(z_ref[r, :], b) + nt(g_ref[r, :], state.astype(BF16))).astype(BF16)
            s_ref[...] = d_ref[pl.ds(c, 1), :] * state + tn(b, x_ref[r, :])
            c = back * per + per - 1 - sub
            r = pl.ds(pl.multiple_of(c * Q, Q), Q)
            state = t_ref[...]
            low = state.astype(BF16)
            tst_ref[c] = low
            q = bc_ref[r, STATE:]
            gb_ref[r, :] = (nn(z_ref[r, :], q) + nt(x_ref[r, :], low)).astype(BF16)
            t_ref[...] = d_ref[pl.ds(c, 1), :] * state + tn(q, g_ref[r, :])
        block_copy(gc_ref, gc_hbm, out_sem, 0, step).start()
        block_copy(gb_ref, gb_hbm, out_sem, 1, back).start()
        block_copy(tst_ref, tst_hbm, out_sem, 2, back, per).start()

    @pl.loop(0, BLOCKS // 2)
    def _(step):
        advance(step, True)

    @pl.loop(BLOCKS // 2, BLOCKS)
    def _(step):
        advance(step, False)

    for i in range(BLOCKS):
        block_copy(gc_ref, gc_hbm, out_sem, 0, i).wait()
        block_copy(gb_ref, gb_hbm, out_sem, 1, i).wait()
        block_copy(tst_ref, tst_hbm, out_sem, 2, i, per).wait()
    ahead.wait()


def chain_call(x, g, bc, sc, z, xt, dec, sp, spf):
    return pl.pallas_call(
        chain_kernel,
        out_shape=(
            far_out((TOK, STATE), BF16),
            far_out((TOK, STATE), BF16),
            far_out((CHUNKS, STATE, WIDTH), BF16),
            kept((TOK, WIDTH), BF16),
        ),
        in_specs=[FAR] * 6 + [WHOLE] * 3,
        out_specs=(FAR, FAR, FAR, WHOLE),
        scratch_shapes=[
            pltpu.VMEM((TOK, WIDTH), BF16),
            pltpu.VMEM((TOK, WIDTH), BF16),
            pltpu.VMEM((TOK, 2 * STATE), BF16),
            pltpu.VMEM((TOK, STATE), BF16),
            pltpu.VMEM((TOK, STATE), BF16),
            pltpu.VMEM((TOK, STATE), BF16),
            pltpu.VMEM((TOK, STATE), BF16),
            pltpu.VMEM((CHUNKS, STATE, WIDTH), BF16),
            pltpu.VMEM((STATE, WIDTH), F32),
            pltpu.VMEM((STATE, WIDTH), F32),
            pltpu.VMEM((CHUNKS, WIDTH), F32),
            pltpu.SemaphoreType.DMA((5, BLOCKS)),
            pltpu.SemaphoreType.DMA((3, BLOCKS)),
            pltpu.SemaphoreType.DMA,
        ],
        compiler_params=options(),
        cost_estimate=cost(4e9, 16e6),
        name="chunk_chain",
    )(*far(x, g, bc, sc, z, xt), dec, sp, spf)


def carry_kernel(place, xt_ref, ge_hbm, gb_hbm, gc_hbm, st_ref, keep_ref, send_ref, ge_ref, gb_ref, gc_ref, in_sem):
    core = place[0]
    loads = ((gb_hbm, gb_ref), (gc_hbm, gc_ref), (ge_hbm, ge_ref))
    for n, (src, dst) in enumerate(loads):
        for i in range(4):
            block_copy(src, dst, in_sem, n, i, 2 * BLOCK).start()
    s = st_ref[:STATE, :]
    t = st_ref[STATE:, :]
    for i in range(4):
        block_copy(gb_hbm, gb_ref, in_sem, 0, i, 2 * BLOCK).wait()
        r = pl.ds(pl.multiple_of((2 * i + core) * BLOCK, BLOCK), BLOCK)
        keep_ref[i, :, :STATE] = gb_ref[r, :] + nt(xt_ref[r, :], t)
        r = pl.ds(pl.multiple_of((2 * i + 1 - core) * BLOCK, BLOCK), BLOCK)
        send_ref[i, :, :STATE] = (gb_ref[r, :] + nt(xt_ref[r, :], t)).astype(BF16)
    for i in range(4):
        block_copy(gc_hbm, gc_ref, in_sem, 1, i, 2 * BLOCK).wait()
        block_copy(ge_hbm, ge_ref, in_sem, 2, i, 2 * BLOCK).wait()
        r = pl.ds(pl.multiple_of((2 * i + core) * BLOCK, BLOCK), BLOCK)
        keep_ref[i, :, STATE:] = gc_ref[r, :] + nt(ge_ref[r, :], s)
        r = pl.ds(pl.multiple_of((2 * i + 1 - core) * BLOCK, BLOCK), BLOCK)
        send_ref[i, :, STATE:] = (gc_ref[r, :] + nt(ge_ref[r, :], s)).astype(BF16)


def carry_call(place, xt, ge, gb, gc, st):
    return pl.pallas_call(
        carry_kernel,
        out_shape=(
            jax.ShapeDtypeStruct((4, BLOCK, 2 * STATE), F32),
            jax.ShapeDtypeStruct((4, BLOCK, 2 * STATE), BF16),
        ),
        in_specs=[SCALARS, WHOLE, FAR, FAR, FAR, WHOLE],
        out_specs=(WHOLE, WHOLE),
        scratch_shapes=[
            pltpu.VMEM((TOK, WIDTH), BF16),
            pltpu.VMEM((TOK, STATE), BF16),
            pltpu.VMEM((TOK, STATE), BF16),
            pltpu.SemaphoreType.DMA((3, 4)),
        ],
        compiler_params=options(),
        cost_estimate=cost(7e8, 9e6),
        name="carry",
    )(place, *held(xt), *far(ge, gb, gc), st)


def input_kernel(
    gx_hbm, tst_hbm, bc_hbm, sc_hbm, st_ref, sp_ref, dec_ref, spf_ref, out_hbm,
    gx_ref, tst_ref, bc_ref, sc_ref, d_ref, in_sem, out_sem,
):
    per = BLOCK // Q
    loads = ((gx_hbm, gx_ref, BLOCK), (tst_hbm, tst_ref, per), (bc_hbm, bc_ref, BLOCK), (sc_hbm, sc_ref, BLOCK))
    for i in range(BLOCKS):
        for n, (src, dst, rows) in enumerate(loads):
            block_copy(src, dst, in_sem, n, i, rows).start()
    d_ref[...] = nn(dec_ref[32 : 32 + CHUNKS, :], spf_ref[...])

    @pl.loop(0, BLOCKS)
    def _(step):
        for n, (src, dst, rows) in enumerate(loads):
            block_copy(src, dst, in_sem, n, step, rows).wait()
        for sub in range(per):
            c = step * per + sub
            r = pl.ds(pl.multiple_of(c * Q, Q), Q)
            full = tst_ref[c].astype(F32) + d_ref[pl.ds(c, 1), :] * st_ref[STATE:, :].astype(F32)
            scale = nn(sc_ref[r, :], sp_ref[:, :WIDTH])
            gx_ref[r, :] = (gx_ref[r, :].astype(F32) + scale * nn(bc_ref[r, :STATE], full.astype(BF16))).astype(BF16)
        block_copy(gx_ref, out_hbm, out_sem, 0, step).start()

    for i in range(BLOCKS):
        block_copy(gx_ref, out_hbm, out_sem, 0, i).wait()


def input_call(gx, tst, st, bc, sc, sp, dec, spf):
    return pl.pallas_call(
        input_kernel,
        out_shape=jax.ShapeDtypeStruct((TOK, WIDTH), BF16),
        in_specs=[FAR] * 4 + [WHOLE] * 4,
        out_specs=FAR,
        scratch_shapes=[
            pltpu.VMEM((TOK, WIDTH), BF16),
            pltpu.VMEM((CHUNKS, STATE, WIDTH), BF16),
            pltpu.VMEM((TOK, 2 * STATE), BF16),
            pltpu.VMEM((TOK, STATE), BF16),
            pltpu.VMEM((CHUNKS, WIDTH), F32),
            pltpu.SemaphoreType.DMA((4, BLOCKS)),
            pltpu.SemaphoreType.DMA((1, BLOCKS)),
        ],
        compiler_params=options(),
        cost_estimate=cost(2e9, 12e6),
        name="input_gradient",
    )(*far(gx, tst, bc, sc), st, sp, dec, spf)


def join_kernel(a_hbm, b_hbm, out_ref, sem):
    loads = [
        pltpu.make_async_copy(a_hbm, out_ref.at[:, :STATE], sem.at[0]),
        pltpu.make_async_copy(b_hbm, out_ref.at[:, STATE:], sem.at[1]),
    ]
    for load in loads:
        load.start()
    for load in loads:
        load.wait()


def join_call(a, b):
    return pl.pallas_call(
        join_kernel,
        out_shape=jax.ShapeDtypeStruct((BLOCK, 2 * STATE), BF16),
        in_specs=[FAR, FAR],
        out_specs=WHOLE,
        scratch_shapes=[pltpu.SemaphoreType.DMA((2,))],
        compiler_params=options(),
        name="join",
    )(*far(a, b))


def pair_kernel(place, keep_ref, got_ref, o0, o1, o2, o3):
    y = place[1]
    for k, o in enumerate((o0, o1, o2, o3)):
        j = lax.rem(y + k, 4)
        o[...] = (keep_ref[j] + got_ref[j].astype(F32)).astype(o.dtype)


def pair_call(place, keep, got):
    return pl.pallas_call(
        pair_kernel,
        out_shape=(jax.ShapeDtypeStruct((BLOCK, 2 * STATE), F32),)
        + (jax.ShapeDtypeStruct((BLOCK, 2 * STATE), BF16),) * 3,
        in_specs=[SCALARS, WHOLE, WHOLE],
        out_specs=(WHOLE,) * 4,
        compiler_params=options(),
        name="pair_sums",
    )(place, keep, got)


def total_kernel(a_ref, b_ref, c_ref, d_ref, w_ref, r_ref):
    t = a_ref[...] + b_ref[...].astype(F32) + c_ref[...].astype(F32) + d_ref[...].astype(F32)
    w_ref[...] = t[:, :STATE]
    r_ref[...] = t[:, STATE:]


def total_call(*parts):
    return pl.pallas_call(
        total_kernel,
        out_shape=(jax.ShapeDtypeStruct((BLOCK, STATE), F32),) * 2,
        compiler_params=options(),
        name="totals",
    )(*parts)


def along_y(k):
    return [(i, (i + 2 * k) % 8) for i in range(8)]


SWAP = [(i, i ^ 1) for i in range(8)]


def shards(mixer_input, write_rows, read_rows, log_decay, skip_gain, reset_offsets, grad_out):
    spot = lax.axis_index("head").astype(jnp.int32)
    core, y = spot & 1, spot >> 1
    place = jnp.stack([core, y])
    me = lax.axis_index("seq").astype(jnp.int32).reshape(1)
    spread_d, spread_c, spread_f = (jnp.asarray(a, BF16) for a in (SPREAD_D, SPREAD_C, SPREAD_F))
    own = join_call(write_rows, read_rows)
    mine = [own] + [lax.ppermute(own, "head", along_y(k)) for k in (1, 2, 3)]
    cum, sc, dec, xt, xt_far, ge = prepare_call(
        reset_offsets, log_decay, jnp.asarray(SUMS, BF16), spread_d, mixer_input, grad_out
    )
    *mine, xt, ge = lax.optimization_barrier((*mine, xt, ge))
    other = [lax.ppermute(a, "head", SWAP) for a in mine]
    payload, bc = state_call(place, mine + other, xt, ge, dec)
    parts = lax.all_to_all(payload, "seq", 0, 0, tiled=True)
    skip = jnp.repeat(skip_gain, 64)[None, :]
    gx, z = within_call(reset_offsets, mixer_input, grad_out, bc, cum, skip)
    parts, gx, z = lax.optimization_barrier((parts, gx, z))
    entering = scan_call(me, parts, spread_f)
    st = lax.all_to_all(entering, "seq", 0, 0, tiled=True).reshape(2 * STATE, WIDTH)
    gc, gb, tst, xt = chain_call(
        mixer_input, grad_out, bc, sc, z, xt_far, dec, spread_c, spread_f
    )
    keep, send = carry_call(place, xt, ge, gb, gc, st)
    total, *leaving = pair_call(place, keep, lax.ppermute(send, "head", SWAP))
    arrived = [lax.ppermute(a, "head", along_y(k)) for k, a in zip((1, 2, 3), leaving)]
    grad_input = input_call(gx, tst, st, bc, sc, spread_c, dec, spread_f)
    return (grad_input, *total_call(total, *arrived))


def solution(mesh):
    in_specs = (
        P("seq", "head"),
        P(("seq", "head"), None),
        P(("seq", "head"), None),
        P("head", "seq"),
        P("head"),
        P("seq", None),
        P("seq", "head"),
    )
    out_specs = (P("seq", "head"), P(("seq", "head"), None), P(("seq", "head"), None))
    return jax.shard_map(shards, mesh=mesh, in_specs=in_specs, out_specs=out_specs, check_vma=False)
```
